256 devices in a mesh: owner: 64 (over z, y, core), view: 4 (over x).
Axes of the slice: x: 4, y: 4, z: 8, core: 2. Of those that a mesh axis runs over, the one named last changes fastest.
Arguments:
- geometry: float32 [4, 5, 2097152], P('view', None, 'owner'), may hold values from -2 to 40, as said below
- appearance: float32 [4, 2097152], P(None, 'owner'), may hold values from -6 to 6, as said below
- list_owner: int32 [4, 262144, 1], P('view', 'owner'), may hold values from 0 to 63; in each aligned block of 4096 rows (0 to 4095, 4096 to 8191, ..., all dimensions but the last counted through in order) at most 128 rows name the same one
- list_local: int32 [4, 262144], P('view', 'owner'), may hold values from 0 to 32767
- counts: int32 [4, 1024], P('view', 'owner'), may hold values from 1 to 256, 131072 in all within a row
- cotangent: float32 [4, 1024, 3, 256], P('view', 'owner'), may hold values from -6 to 6
Outputs:
- geo_grad: float32 [4, 5, 2097152], P('view', None, 'owner')
- look_grad: float32 [4, 2097152], P(None, 'owner')
The draws below stay inside these ranges and needn't reach their ends.
Inputs may be any that keep to these rules, and one draw needn't show every extreme that they name: `list_owner`: within the slots of one device's tiles (4096 slots in a row of one view), no owner is named more than 128 times, a bound that some block reaches. `geometry`: rows 0 and 1 lie in [0, 1], rows 2 and 4 in [4, 40], row 3 in [-2, 2]. `appearance`: rows 0 to 2 lie in [-6, 6], row 3 in [-6, -1.5].
All inputs are finite; a program needn't handle non-finite values. No bound on the sum of `counts` on one device may be relied on, other than what follows from the above.
Results may differ from the reference program's by a relative error of at most 0.0003.
Values sent between devices are 32-bit elements; how exact they have to be, the bound alone decides.
No kernel may reach another device: no remote copies, remote signals or barrier semaphores. Data moves between devices by JAX's collectives and lax.ppermute only.
A program may use at most 192 MiB of HBM per device.

```python
import math
import jax
import jax.numpy as jnp
import numpy as np
from jax import lax

TILE_DEV = 16
G_DEV = 32768
K = 256
TS = 16
P_SIZE = 256
VIEWS = 4
TILES = 1024
GAUSS = 2097152
CAP = 128
N_OWNER = 64


def draw_geometry(key, part):
    key = jax.random.fold_in(key, 11)
    keys = jax.random.split(key, 5)
    shape = (VIEWS, GAUSS)
    center_x = jax.random.uniform(keys[0], shape, jnp.float32, 0.0, 1.0)
    center_y = jax.random.uniform(keys[1], shape, jnp.float32, 0.0, 1.0)
    conic_a = jax.random.uniform(keys[2], shape, jnp.float32, 4.0, 40.0)
    conic_c = jax.random.uniform(keys[4], shape, jnp.float32, 4.0, 40.0)
    conic_b = jax.random.uniform(keys[3], shape, jnp.float32, -2.0, 2.0)
    return jnp.stack([center_x, center_y, conic_a, conic_b, conic_c], axis=1)


def draw_appearance(key, part):
    key = jax.random.fold_in(key, 12)
    keys = jax.random.split(key, 2)
    colors = jnp.clip(jax.random.normal(keys[0], (3, GAUSS), jnp.float32), -6.0, 6.0)
    opacity = jax.random.uniform(keys[1], (1, GAUSS), jnp.float32, -5.0, -2.0)
    return jnp.concatenate([colors, opacity], 0)


def place_ends(result, rng, smallest, largest):
    extent = result.shape
    index_at = [jax.random.randint(jax.random.fold_in(rng, axis), (), 0, extent[axis]) for axis in range(len(extent))]
    result = result.at[tuple(index_at)].set(smallest)
    longest = extent.index(max(extent))
    index_at[longest] = (index_at[longest] + 1) % extent[longest]
    return result.at[tuple(index_at)].set(largest)


def shard_levels(key, shape, cuts, least, top_value):
    loudness, own = 1.0, jax.random.fold_in(key, 6)
    for axis_at, parts in cuts:
        heights = jnp.exp(jax.random.uniform(jax.random.fold_in(own, axis_at), (parts,), jnp.float32, least / len(cuts), top_value / len(cuts)))
        loudness = loudness * jnp.repeat(heights, shape[axis_at] // parts).reshape([-1 if axis == axis_at else 1 for axis in range(len(shape))])
    return loudness


def profile(amount, total, reach, skew):
    loads = [(1 << 20) // math.isqrt(rank ** skew) + 1 for rank in range(2, amount + 1)]
    spare, holding = total - reach - (amount - 1), [1] * (amount - 1)
    while spare > 0:
        movable = [i for i in range(amount - 1) if holding[i] < reach]
        whole, remaining = sum([loads[i] for i in movable]), spare
        for i in movable:
            more = min(reach - holding[i], max(1, remaining * loads[i] // whole), spare)
            holding[i] = holding[i] + more
            spare = spare - more
    return np.array([reach] + holding)


def ragged_sizes(rng, amount, total, limit, skew):
    if amount == 2:
        one = jax.random.randint(rng, (), max(1, total - limit), min(limit, total - 1) + 1)
        return jnp.stack([one, total - one])
    sizes = jnp.asarray(profile(amount, total, limit, skew), jnp.int32)
    pairs = (amount - 1) // 2
    giver, taker = sizes[1:1 + 2 * pairs:2], sizes[2:2 + 2 * pairs:2]
    slack = jnp.minimum(giver - 1, limit - taker)
    shifted = jax.random.randint(jax.random.fold_in(rng, 1), (pairs,), 0, 1 << 20) % (slack + 1)
    sizes = sizes.at[1:1 + 2 * pairs:2].set(giver - shifted).at[2:2 + 2 * pairs:2].set(taker + shifted)
    return sizes[jax.random.permutation(jax.random.fold_in(rng, 2), amount)]


def assign_block(own_key, own, number, rows, amount, top, reach, slope):
    order = jax.random.permutation(own_key, amount)
    crowded, usual = portions_of(amount, rows * top, reach, slope, True), portions_of(amount, rows * top, reach, slope, False)
    places = jnp.arange(amount)

    def named(sizes, rotation):
        used = int((sizes > 0).sum())
        fixed = max(1, used // 4)
        moved = fixed + (places - fixed + rotation * (used - fixed)) % max(1, amount - fixed)
        return jnp.zeros((amount,), jnp.int32).at[order[jnp.where(places < fixed, places, moved)]].set(jnp.asarray(sizes, jnp.int32))

    sizes = jnp.where(number % 4 == 0, named(crowded, number // 4), named(usual, number - number // 4 - 1))
    mixed = jax.random.permutation(jax.random.fold_in(own, 3), amount)
    source_of, receiver = mixed[0:amount // 2 * 2:2], mixed[1:amount // 2 * 2:2]
    margin = jnp.minimum(sizes[source_of] - 1, reach - sizes[receiver]) // 2
    margin = jnp.where((source_of == order[0]) | (receiver == order[0]) | (sizes[receiver] == 0), 0, jnp.maximum(margin, 0))
    moved = jax.random.randint(jax.random.fold_in(own, 4), (amount // 2,), 0, 1 << 20) % (margin + 1)
    sizes = sizes.at[source_of].add(-moved).at[receiver].add(moved)
    labels = jnp.searchsorted(jnp.cumsum(sizes), jnp.arange(rows * top), side="right").astype(jnp.int32)
    grid = labels.reshape(top, rows).T
    grid = grid[jax.random.permutation(jax.random.fold_in(own, 1), rows)]
    rotation = jax.random.randint(jax.random.fold_in(own, 2), (rows, 1), 0, top)
    return jnp.take_along_axis(grid, (jnp.arange(top)[None, :] + rotation) % top, axis=1)


def portions_of(amount, total, limit, skew, full):
    weights = [(1 << 20) // math.isqrt(grade ** skew) + 1 for grade in range(1, amount + 1)]
    largest = limit if full else min(limit, max(-(-total // amount), total * weights[0] // sum(weights)))
    least = 1 if total - largest >= amount - 1 else 0
    holding, surplus = [largest] + [least] * (amount - 1), total - largest - least * (amount - 1)
    while surplus > 0:
        candidates = [i for i in range(1, amount) if holding[i] < largest] or [i for i in range(1, amount) if holding[i] < limit]
        mass, budget = sum([weights[i] for i in candidates]), surplus
        for i in candidates:
            extra = min(limit - holding[i], max(1, budget * weights[i] // mass), surplus)
            holding[i] = holding[i] + extra
            surplus = surplus - extra
    return np.array(holding)


def noise(own_key, shape, deviation, reach, pieces=(), held_as=jnp.bfloat16):
    level = shard_levels(own_key, shape, pieces, -0.22, 0.18) if pieces else 1.0
    array = jax.random.normal(own_key, shape, jnp.float32) * deviation * level
    return jnp.minimum(jnp.maximum(array, -reach), reach).astype(held_as)


def setup_inputs(seed: int = 0) -> dict:
    seeds = jax.random.split(jax.random.key(seed), 7)
    geometry = draw_geometry(jax.random.fold_in(seeds[6], 71), 0)
    appearance = draw_appearance(jax.random.fold_in(seeds[6], 71), 0)
    list_owner_keys = jax.random.split(jax.random.fold_in(seeds[2], 1), VIEWS * (TILES * K) // (TILE_DEV * K))
    list_owner_turns = jax.random.permutation(jax.random.fold_in(seeds[2], 3), VIEWS * (TILES * K) // (TILE_DEV * K))
    list_owner = jax.vmap(lambda own, number: assign_block(jax.random.fold_in(seeds[2], 2), own, number, TILE_DEV * K, N_OWNER, 1, CAP, 2))(list_owner_keys, list_owner_turns).reshape((VIEWS, TILES * K, 1))
    list_local = place_ends(jax.random.randint(seeds[3], (VIEWS, TILES * K), 0, G_DEV), jax.random.fold_in(seeds[3], 1), 0, G_DEV - 1).astype(jnp.int32)
    counts = jax.vmap(lambda own: ragged_sizes(own, TILES, TILES * K // 2, K, 2))(jax.random.split(seeds[4], VIEWS)).reshape((VIEWS, TILES)).astype(jnp.int32)
    cotangent = noise(seeds[5], (VIEWS, TILES, 3, P_SIZE), 1.0, 6.0, ((0, 4), (1, 64)), jnp.float32)
    return dict(geometry=geometry, appearance=appearance, list_owner=list_owner, list_local=list_local, counts=counts, cotangent=cotangent)


def running_prefix(log_keep):
    return jnp.cumsum(log_keep, axis=1) - log_keep

def render(entries, alive, pixel_x, pixel_y):
    offset_x = pixel_x[:, None] - entries[0][None, :]
    offset_y = pixel_y[:, None] - entries[1][None, :]
    falloff = 0.5 * (entries[2][None, :] * offset_x * offset_x + 2.0 * entries[3][None, :] * offset_x * offset_y + entries[4][None, :] * offset_y * offset_y)
    alphas = 0.99 * jax.nn.sigmoid(entries[8])[None, :] * jnp.exp(-falloff) * alive[None, :]
    log_keep = jnp.log1p(-alphas)
    transmit = jnp.exp(running_prefix(log_keep))
    weight = transmit * alphas
    return jnp.dot(entries[5:8], weight.T, precision=lax.Precision.HIGHEST)

def tile_grad(entries, alive, tile_cot, pixel_x, pixel_y):
    colors, pullback = jax.vjp(lambda values: render(values, alive, pixel_x, pixel_y), entries)
    return pullback(tile_cot)[0]

def reference(geometry, appearance, list_owner, list_local, counts, cotangent):
    pixel = jnp.arange(TS * TS, dtype=jnp.int32)
    pixel_x = ((pixel % TS).astype(jnp.float32) + 0.5) / TS
    pixel_y = ((pixel // TS).astype(jnp.float32) + 0.5) / TS
    geo_list = []
    look_grad = jnp.zeros((4, GAUSS), jnp.float32)
    for camera in range(VIEWS):
        gauss_ids = (list_owner[camera, :, 0] * G_DEV + list_local[camera]).astype(jnp.int32)
        tiled_ids = gauss_ids.reshape(TILES, K)
        stacked = jnp.concatenate([geometry[camera][:, tiled_ids], appearance[:, tiled_ids]], 0)
        stacked = jnp.transpose(stacked, (1, 0, 2))
        alive = (jnp.arange(K, dtype=jnp.int32)[None, :] < counts[camera][:, None]).astype(jnp.float32)
        gradients = lax.map(lambda packed: tile_grad(packed[0], packed[1], packed[2], pixel_x, pixel_y), (stacked, alive, cotangent[camera]))
        flattened = jnp.transpose(gradients, (1, 0, 2)).reshape(9, TILES * K)
        geo_list.append(jnp.zeros((5, GAUSS), jnp.float32).at[:, gauss_ids].add(flattened[:5]))
        look_grad = look_grad.at[:, gauss_ids].add(flattened[5:])
    return (jnp.stack(geo_list), look_grad)
```

```python
import functools

import jax
import jax.numpy as jnp
from jax import lax
from jax.experimental import pallas as pl
from jax.experimental.pallas import tpu as pltpu
from jax.sharding import PartitionSpec as P

K = 256
TS = 16
LANES = 128
LOW = 64
F32 = jnp.float32
BF16 = jnp.bfloat16
LOG2E = 1.4426950408889634


def split2(x):
    high = x.astype(BF16)
    return high, (x - high.astype(F32)).astype(BF16)


def split3(x):
    high = x.astype(BF16)
    rest = x - high.astype(F32)
    middle = rest.astype(BF16)
    return high, middle, (rest - middle.astype(F32)).astype(BF16)


def dot_nn(a, b):
    return lax.dot_general(a, b, (((1,), (0,)), ((), ())), preferred_element_type=F32)


def dot_nt(a, b):
    return lax.dot_general(a, b, (((1,), (1,)), ((), ())), preferred_element_type=F32)


def row_iota(rows, columns):
    return lax.broadcasted_iota(jnp.int32, (rows, columns), 0)


def lane_iota(rows, columns):
    return lax.broadcasted_iota(jnp.int32, (rows, columns), 1)


def named_mask(owner_row, count, owners):
    live = lane_iota(1, K) < count
    shown = jnp.where(live, owner_row, -1)
    return row_iota(owners, K) == shown


def plan_kernel(counts_ref, owner_ref, local_ref, request_ref, rank_ref):
    tiles = owner_ref.shape[0]
    owners = request_ref.shape[0]
    before = (row_iota(K, K) < lane_iota(K, K)).astype(BF16)
    carry = jnp.zeros((owners, 1), F32)
    total = jnp.zeros((owners, 2 * LANES), F32)
    for t in range(tiles):
        named = named_mask(owner_ref[t : t + 1, :], counts_ref[0, t], owners).astype(F32)
        named_half = named.astype(BF16)
        inside = dot_nn(named_half, before)
        rank = jnp.sum(named * (inside + carry), axis=0, keepdims=True).astype(jnp.int32)
        carry = carry + jnp.sum(named, axis=1, keepdims=True)
        rank_ref[t : t + 1, :] = rank
        ids = local_ref[t : t + 1, :] + 1
        at_rank = row_iota(LANES, K) == rank
        high = jnp.where(at_rank, (ids >> 7).astype(F32), 0.0).astype(BF16)
        low = jnp.where(at_rank, (ids & 127).astype(F32), 0.0).astype(BF16)
        total = total + dot_nt(named_half, jnp.concatenate([high, low], 0))
    request_ref[...] = (total[:, :LANES] * 128.0 + total[:, LANES:]).astype(jnp.int32) - 1


def pair_row(ref, at):
    both = ref[pl.ds(at, 2), :]
    return jnp.concatenate([both[0:1, :], both[1:2, :]], 1)


def high_part(ids):
    part = (ids >> 7) + jnp.where((ids & LOW) != 0, 256, 0)
    return jnp.where(ids < 0, -1, part)


def gather_kernel(ids_ref, geo_ref, app_ref, out_ref, table_ref):
    owners = ids_ref.shape[0]
    for c in range(9):
        values = geo_ref[c] if c < 5 else app_ref[c - 5]
        high, low = split2(values.T)
        table_ref[c * LOW : (c + 1) * LOW, :] = jnp.concatenate(
            [high[:LOW], high[LOW:], low[:LOW], low[LOW:]], 1
        )

    def group(g, _):
        blocks = []
        for j in range(4):
            ids = pair_row(ids_ref, pl.multiple_of(g * 8, 8) + 2 * j)
            hot = (row_iota(512, 256) == high_part(ids)).astype(F32).astype(BF16)
            found = dot_nn(table_ref[...], jnp.concatenate([hot, hot], 0))
            mask = row_iota(LOW, 256) == (ids & (LOW - 1))
            rows = [
                jnp.sum(jnp.where(mask, found[c * LOW : (c + 1) * LOW], 0.0), axis=0, keepdims=True)
                for c in range(9)
            ]
            values = jnp.concatenate(rows, 0)
            blocks += [values[:, :LANES], values[:, LANES:]]
        out_ref[pl.ds(pl.multiple_of(g * 72, 8), 72), :] = jnp.concatenate(blocks, 0)
        return 0

    lax.fori_loop(0, owners // 8, group, 0)


def pixel_rows():
    pixel = lane_iota(1, K)
    u = ((pixel & (TS - 1)).astype(F32) + 0.5) / TS - 0.5
    v = ((pixel >> 4).astype(F32) + 0.5) / TS - 0.5
    one = jnp.ones((1, K), F32)
    zero = jnp.zeros((2, K), F32)
    return jnp.concatenate([u * u, u * v, v * v, u, v, one, zero], 0)


def tile_kernel(
    counts_ref, owner_ref, rank_ref, cot_ref, fetched_ref, out_ref, table_ref, grad_ref, dots_ref
):
    tiles = owner_ref.shape[0]
    owners = fetched_ref.shape[0] // 9
    for c in range(9):
        high, low = split2(fetched_ref[pl.ds(c, owners, stride=9), :])
        table_ref[c * owners : (c + 1) * owners, :] = jnp.concatenate([high, low], 1)
    grad_ref[...] = jnp.zeros_like(grad_ref)
    pixels = pixel_rows()
    monomials = pixels.astype(BF16)
    pixel_columns = jnp.concatenate([pixels] * 4, 0).T.astype(BF16)
    before = (row_iota(K, K) < lane_iota(K, K)).astype(BF16)
    after = (row_iota(K, K) > lane_iota(K, K)).astype(BF16)
    dots_ref[0:K] = before
    dots_ref[K : 2 * K] = before
    dots_ref[2 * K : 3 * K] = after
    dots_ref[3 * K : 4 * K] = after

    def one_tile(t, _):
        named = named_mask(owner_ref[pl.ds(t, 1), :], counts_ref[0, t], owners)
        at_rank = (row_iota(LANES, K) == rank_ref[pl.ds(t, 1), :]).astype(F32).astype(BF16)
        spread = dot_nn(table_ref[...], jnp.concatenate([at_rank, at_rank], 0))
        entries = [
            jnp.sum(
                jnp.where(named, spread[c * owners : (c + 1) * owners], 0.0), axis=0, keepdims=True
            )
            for c in range(9)
        ]
        cx, cy, a, b, c2 = entries[0] - 0.5, entries[1] - 0.5, entries[2], entries[3], entries[4]
        opacity = 1.0 / (1.0 + jnp.exp(-entries[8]))
        live = lane_iota(1, K) < counts_ref[0, t]
        ax, ay = a * cx + b * cy, b * cx + c2 * cy
        base = jnp.log(0.99 * opacity) * LOG2E - (0.5 * LOG2E) * (ax * cx + ay * cy)
        zero = jnp.zeros((2, K), F32)
        coefs = jnp.concatenate(
            [
                (-0.5 * LOG2E) * a,
                -LOG2E * b,
                (-0.5 * LOG2E) * c2,
                LOG2E * ax,
                LOG2E * ay,
                jnp.where(live, base, -400.0),
                zero,
            ],
            0,
        )
        parts = split3(coefs)
        exponent = dot_nn(
            pixel_columns, jnp.concatenate([*parts, jnp.zeros((8, K), BF16)], 0)
        )
        alphas = jnp.exp2(exponent)
        log_keep = jnp.log(1.0 - alphas)
        prefix = dot_nn(jnp.concatenate(split2(log_keep), 1), dots_ref[0 : 2 * K])
        weight = jnp.exp(prefix) * alphas
        cot_high, cot_low = split2(cot_ref[t])
        ch, cl = cot_high.astype(F32), cot_low.astype(F32)
        pad = jnp.zeros((4, K), F32)
        cot_columns = jnp.concatenate([ch, ch, cl, cl, pad], 0).T.astype(BF16)
        colors = jnp.concatenate(entries[5:8], 0)
        color_high, color_low = split2(colors)
        kh, kl = color_high.astype(F32), color_low.astype(F32)
        slopes = dot_nn(cot_columns, jnp.concatenate([kh, kl, kh, kl, pad], 0).astype(BF16))
        pull = weight * slopes
        suffix = dot_nn(jnp.concatenate(split2(pull), 1), dots_ref[2 * K : 4 * K])
        q = pull - alphas * jnp.exp(-log_keep) * suffix
        q_high, q_low = split2(q)
        moments = dot_nn(monomials, q_high) + dot_nn(monomials, q_low)
        w_high, w_low = split2(weight)
        cot_rows = jnp.concatenate([ch, cl, jnp.zeros((2, K), F32)], 0).astype(BF16)
        tints = dot_nn(cot_rows, w_high) + dot_nn(cot_rows, w_low)
        tints = tints[0:3] + tints[3:6]
        mxx, mxy, myy, mx, my, m0 = [moments[i : i + 1] for i in range(6)]
        sx, sy = mx - cx * m0, my - cy * m0
        sxx = mxx - cx * (mx + sx)
        sxy = mxy - cx * my - cy * sx
        syy = myy - cy * (my + sy)
        rows = [
            a * sx + b * sy,
            b * sx + c2 * sy,
            -0.5 * sxx,
            -sxy,
            -0.5 * syy,
            tints[0:1],
            tints[1:2],
            tints[2:3],
            (1.0 - opacity) * m0,
        ]
        placed = []
        for row in rows:
            row_high = row.astype(BF16).astype(F32)
            high = jnp.where(named, row_high, 0.0).astype(BF16)
            low = jnp.where(named, row - row_high, 0.0).astype(BF16)
            placed.append(jnp.concatenate([high, low], 1))
        grad_ref[...] += dot_nt(
            jnp.concatenate(placed, 0), jnp.concatenate([at_rank, at_rank], 1)
        )
        return 0

    lax.fori_loop(0, tiles, one_tile, 0)
    for c in range(9):
        out_ref[pl.ds(c, owners, stride=9), :] = grad_ref[c * owners : (c + 1) * owners, :]


def scatter_kernel(first, number, ids_ref, vals_ref, out_ref, acc_ref):
    owners = ids_ref.shape[0]
    acc_ref[...] = jnp.zeros_like(acc_ref)

    def group(g, _):
        values = vals_ref[pl.ds(pl.multiple_of(g * 72, 8), 72), :]
        sides, hots = [], []
        for j in range(4):
            ids = pair_row(ids_ref, pl.multiple_of(g * 8, 8) + 2 * j)
            hot = (row_iota(512, 256) == high_part(ids)).astype(F32).astype(BF16)
            mask = row_iota(LOW, 256) == (ids & (LOW - 1))
            stacked = []
            for c in range(first, first + number):
                at = 18 * j + c
                row = jnp.concatenate([values[at : at + 1], values[at + 9 : at + 10]], 1)
                row_high = row.astype(BF16).astype(F32)
                high = jnp.where(mask, row_high, 0.0).astype(BF16)
                low = jnp.where(mask, row - row_high, 0.0).astype(BF16)
                stacked.append(jnp.concatenate([high, low], 1))
            sides.append(jnp.concatenate(stacked, 0))
            hots += [hot, hot]
        acc_ref[...] += dot_nt(jnp.concatenate(sides, 1), jnp.concatenate(hots, 1))
        return 0

    lax.fori_loop(0, owners // 8, group, 0)
    for c in range(number):
        part = acc_ref[c * LOW : (c + 1) * LOW, :]
        out_ref[c] = jnp.concatenate([part[:, :256], part[:, 256:]], 0).T


VMEM = pl.BlockSpec(memory_space=pltpu.VMEM)
SMEM = pl.BlockSpec(memory_space=pltpu.SMEM)
LIMIT = pltpu.CompilerParams(vmem_limit_bytes=40 * 1024 * 1024)


def exchange(values, owners, axis="owner"):
    sent = values.reshape(owners, 1, -1)
    got = lax.all_to_all(sent, axis, split_axis=0, concat_axis=0, tiled=True)
    return got.reshape(values.shape)


def shards(geometry, appearance, list_owner, list_local, counts, cotangent):
    owners = lax.axis_size("owner")
    tiles = counts.shape[1]
    gauss = geometry.shape[2]
    target = list_owner.reshape(tiles, K)
    local = list_local.reshape(tiles, K)
    requests, ranks = pl.pallas_call(
        plan_kernel,
        out_shape=(
            jax.ShapeDtypeStruct((owners, LANES), jnp.int32),
            jax.ShapeDtypeStruct((tiles, K), jnp.int32),
        ),
        in_specs=[SMEM, VMEM, VMEM],
        out_specs=(VMEM, VMEM),
        compiler_params=LIMIT,
    )(counts, target, local)
    ids = exchange(requests, owners)
    picked = pl.pallas_call(
        gather_kernel,
        out_shape=jax.ShapeDtypeStruct((owners * 9, LANES), F32),
        in_specs=[VMEM, VMEM, VMEM],
        out_specs=VMEM,
        scratch_shapes=[pltpu.VMEM((9 * LOW, 1024), BF16)],
        compiler_params=LIMIT,
    )(ids, geometry.reshape(5, gauss // LANES, LANES), appearance.reshape(4, gauss // LANES, LANES))
    fetched = exchange(picked, owners)
    outgoing = pl.pallas_call(
        tile_kernel,
        out_shape=jax.ShapeDtypeStruct((owners * 9, LANES), F32),
        in_specs=[SMEM, VMEM, VMEM, VMEM, VMEM],
        out_specs=VMEM,
        scratch_shapes=[
            pltpu.VMEM((9 * owners, 2 * LANES), BF16),
            pltpu.VMEM((9 * owners, LANES), F32),
            pltpu.VMEM((4 * K, K), BF16),
        ],
        compiler_params=LIMIT,
    )(counts, target, ranks, cotangent[0], fetched)
    returned = exchange(outgoing, owners)

    def scatter(first, number):
        return pl.pallas_call(
            functools.partial(scatter_kernel, first, number),
            out_shape=jax.ShapeDtypeStruct((number, gauss // LANES, LANES), F32),
            in_specs=[VMEM, VMEM],
            out_specs=VMEM,
            scratch_shapes=[pltpu.VMEM((number * LOW, 512), F32)],
            compiler_params=LIMIT,
        )(ids, returned)

    look = lax.psum(scatter(5, 4), "view")
    geo = scatter(0, 5)
    return (geo.reshape(1, 5, gauss), look.reshape(4, gauss))


def solution(mesh):
    placed = (
        P("view", None, "owner"),
        P(None, "owner"),
        P("view", "owner", None),
        P("view", "owner"),
        P("view", "owner"),
        P("view", "owner", None, None),
    )
    return jax.shard_map(
        shards,
        mesh=mesh,
        in_specs=placed,
        out_specs=(P("view", None, "owner"), P(None, "owner")),
        check_vma=False,
    )
```

```python
import functools
import math

import jax
import jax.numpy as jnp
from jax import lax
from jax.experimental import pallas as pl
from jax.experimental.pallas import tpu as pltpu
from jax.sharding import PartitionSpec as P

K = 256
TS = 16
LANES = 128
LOW = 64
F32 = jnp.float32
BF16 = jnp.bfloat16
LOG2E = 1.4426950408889634


def split2(x):
    high = x.astype(BF16)
    return high, (x - high.astype(F32)).astype(BF16)


def split3(x):
    high = x.astype(BF16)
    rest = x - high.astype(F32)
    middle = rest.astype(BF16)
    return high, middle, (rest - middle.astype(F32)).astype(BF16)


def dot_nn(a, b):
    return lax.dot_general(a, b, (((1,), (0,)), ((), ())), preferred_element_type=F32)


def dot_nt(a, b):
    return lax.dot_general(a, b, (((1,), (1,)), ((), ())), preferred_element_type=F32)


def row_iota(rows, columns):
    return lax.broadcasted_iota(jnp.int32, (rows, columns), 0)


def lane_iota(rows, columns):
    return lax.broadcasted_iota(jnp.int32, (rows, columns), 1)


def named_mask(owner_row, count, owners):
    live = lane_iota(1, K) < count
    shown = jnp.where(live, owner_row, -1)
    return row_iota(owners, K) == shown


def plan_kernel(counts_ref, owner_ref, local_ref, request_ref, rank_ref):
    tiles = rank_ref.shape[0]
    owners = request_ref.shape[0]
    before = (row_iota(K, K) < lane_iota(K, K)).astype(BF16)
    carry = jnp.zeros((owners, 1), F32)
    total = jnp.zeros((owners, 2 * LANES), F32)
    for t in range(tiles):
        at = slice(t * K, (t + 1) * K)
        named = named_mask(owner_ref[:, at], counts_ref[0, t], owners).astype(F32)
        named_half = named.astype(BF16)
        inside = dot_nn(named_half, before)
        rank = jnp.sum(named * (inside + carry), axis=0, keepdims=True).astype(jnp.int32)
        carry = carry + jnp.sum(named, axis=1, keepdims=True)
        rank_ref[t : t + 1, :] = rank
        ids = local_ref[:, at] + 1
        hits = hits16(LANES, rank)
        high = keep16(hits, (ids >> 7).astype(F32).astype(BF16))
        low = keep16(hits, (ids & 127).astype(F32).astype(BF16))
        total = total + dot_nt(named_half, jnp.concatenate([high, low], 0))
    request_ref[...] = (total[:, :LANES] * 128.0 + total[:, LANES:]).astype(jnp.int32)


def table_kernel(geo_ref, app_ref, table_ref):
    for c in range(9):
        values = geo_ref[c] if c < 5 else app_ref[c - 5]
        high, low = split2(values.T)
        table_ref[c * LOW : (c + 1) * LOW, :] = jnp.concatenate(
            [high[:LOW], high[LOW:], low[:LOW], low[LOW:]], 1
        )


WIDE = 8


def ids_row(ref, at):
    return jnp.concatenate([ref[pl.ds(at, 1), :], ref[pl.ds(at + 1, 1), :]], 1) - 1


def hits16(rows, row):
    return lax.broadcasted_iota(jnp.int16, (rows, row.shape[1]), 0) == row.astype(jnp.int16)


def keep16(hits, row):
    return jnp.where(hits, row, jnp.zeros_like(row))


def hot16(rows, row):
    return keep16(hits16(rows, row), jnp.ones((rows, row.shape[1]), BF16))


def hot_rows(ids):
    part = (ids >> 7) + jnp.where((ids & LOW) != 0, 256, 0)
    part = jnp.where(ids < 0, -1, part)
    return hot16(512, part)


def low_mask(ids):
    return row_iota(LOW, 256) == (ids & (LOW - 1))


def chunks_of(total):
    return (total + WIDE * LANES - 1) // (WIDE * LANES)


def merge(now, rolled, offset, following):
    fits = lane_iota(*now.shape) >= (offset & 127)
    block = now + jnp.where(fits, rolled, jnp.zeros_like(rolled))
    spilt = jnp.where(fits, jnp.zeros_like(rolled), rolled)
    return block, jnp.where((following >> 7) > (offset >> 7), spilt, block)


def gather_kernel(
    asked_ref, table_ref, out_ref, packed_ref, place_ref, found_ref, sem
):
    owners = asked_ref.shape[0]
    valid = (asked_ref[...] > 0).astype(F32).astype(BF16)
    earlier = (row_iota(owners, owners) > lane_iota(owners, owners)).astype(F32).astype(BF16)
    ones = jnp.ones((8, LANES), BF16)
    offsets = dot_nt(ones, dot_nn(earlier, valid).astype(BF16))
    amounts = dot_nt(ones, valid)
    packed_ref[0:owners, :] = jnp.zeros((owners, LANES), jnp.int32)
    place = jnp.concatenate([offsets, amounts], 1).astype(jnp.int32)
    packed_ref[owners : owners + 8, 0 : 2 * owners] = place
    copy = pltpu.make_async_copy(packed_ref.at[pl.ds(owners, 8), :], place_ref, sem)
    copy.start()
    copy.wait()
    total = place_ref[0, owners - 1] + place_ref[0, 2 * owners - 1]

    def compact(g, now):
        for j in range(8):
            s = g * 8 + j
            offset = place_ref[0, s]
            following = offset + place_ref[0, owners + s]
            row = jnp.broadcast_to(asked_ref[pl.ds(s, 1), :], (8, LANES))
            rolled = pltpu.roll(row, offset & 127, 1)
            block, now = merge(now, rolled, offset, following)
            packed_ref[pl.ds(offset >> 7, 1), :] = block[0:1]
        return now

    now = lax.fori_loop(0, owners // 8, compact, jnp.zeros((8, LANES), jnp.int32))

    @pl.when(total < owners * LANES)
    def _():
        packed_ref[pl.ds(total >> 7, 1), :] = now[0:1]

    def chunk(j, _):
        for at in range(0, WIDE, 2):
            ids = ids_row(packed_ref, WIDE * j + at)
            hot = hot_rows(ids)
            found = dot_nn(table_ref[...], jnp.concatenate([hot, hot], 0))
            mask = low_mask(ids)
            rows = [
                jnp.sum(jnp.where(mask, found[c * LOW : (c + 1) * LOW], 0.0), axis=0, keepdims=True)
                for c in range(9)
            ]
            values = jnp.concatenate(rows, 0)
            found_ref[WIDE * j + at, 0:9, :] = values[:, :LANES]
            found_ref[WIDE * j + at + 1, 0:9, :] = values[:, LANES:]
        return 0

    lax.fori_loop(0, chunks_of(total), chunk, 0)

    def expand(g, _):
        blocks = []
        for j in range(8):
            s = g * 8 + j
            offset, amount = place_ref[0, s], place_ref[0, owners + s]
            here, back = offset >> 7, (LANES - (offset & 127)) & 127
            first = pltpu.roll(found_ref[here], back, 1)
            second = pltpu.roll(found_ref[here + 1], back, 1)
            lanes = lane_iota(16, LANES)
            values = jnp.where(lanes + (offset & 127) < LANES, first, second)
            blocks.append(jnp.where(lanes < amount, values, 0.0)[0:9])
        out_ref[pl.ds(pl.multiple_of(g * 72, 8), 72), :] = jnp.concatenate(blocks, 0)
        return 0

    lax.fori_loop(0, owners // 8, expand, 0)


def pixel_rows():
    pixel = lane_iota(1, K)
    u = ((pixel & (TS - 1)).astype(F32) + 0.5) / TS - 0.5
    v = ((pixel >> 4).astype(F32) + 0.5) / TS - 0.5
    one = jnp.ones((1, K), F32)
    zero = jnp.zeros((2, K), F32)
    return jnp.concatenate([u * u, u * v, v * v, u, v, one, zero], 0)


def tile_kernel(
    unrolls,
    counts_ref,
    owner_ref,
    rank_ref,
    cot_ref,
    fetched_ref,
    out_ref,
    table_ref,
    grad_ref,
    dots_ref,
    entry_ref,
    coef_ref,
    sums_ref,
):
    tiles = rank_ref.shape[0]
    owners = fetched_ref.shape[0] // 9
    unrolls = [math.gcd(tiles, n) for n in unrolls]
    for c in range(9):
        high, low = split2(fetched_ref[pl.ds(c, owners, stride=9), :])
        table_ref[c * owners : (c + 1) * owners, :] = jnp.concatenate([high, low], 1)
    grad_ref[...] = jnp.zeros_like(grad_ref)
    pixels = pixel_rows()
    monomials = pixels.astype(BF16)
    pixel_columns = jnp.concatenate([pixels] * 4, 0).T.astype(BF16)
    before = (row_iota(K, K) < lane_iota(K, K)).astype(BF16)
    after = (row_iota(K, K) > lane_iota(K, K)).astype(BF16)
    dots_ref[0:K] = before
    dots_ref[K : 2 * K] = before
    dots_ref[2 * K : 3 * K] = after
    dots_ref[3 * K : 4 * K] = after

    def owner_row(t):
        row = owner_ref[:, pl.ds(pl.multiple_of(t * K, K), K)]
        return jnp.where(lane_iota(1, K) < counts_ref[0, t], row, -1)

    def fetch(g, _):
        several = [unrolls[0] * g + i for i in range(unrolls[0])]
        hots = [hot16(LANES, rank_ref[pl.ds(t, 1), :]) for t in several]
        spreads = [dot_nn(table_ref[...], jnp.concatenate([hot, hot], 0)) for hot in hots]
        for t, spread in zip(several, spreads):
            named = row_iota(owners, K) == owner_row(t)
            for c in range(9):
                kept = jnp.where(named, spread[c * owners : (c + 1) * owners], 0.0)
                entry_ref[c, pl.ds(t, 1), :] = jnp.sum(kept, axis=0, keepdims=True)
        return 0

    lax.fori_loop(0, tiles // unrolls[0], fetch, 0)
    cx, cy = entry_ref[0] - 0.5, entry_ref[1] - 0.5
    a, b, c2 = entry_ref[2], entry_ref[3], entry_ref[4]
    opacity = 1.0 / (1.0 + jnp.exp(-entry_ref[8]))
    spots = lane_iota(1, K)
    left = jnp.concatenate([counts_ref[0, t] - spots for t in range(tiles)], 0)
    ax, ay = a * cx + b * cy, b * cx + c2 * cy
    base = jnp.log(0.99 * opacity) * LOG2E - (0.5 * LOG2E) * (ax * cx + ay * cy)
    coefs = [
        (-0.5 * LOG2E) * a,
        -LOG2E * b,
        (-0.5 * LOG2E) * c2,
        LOG2E * ax,
        LOG2E * ay,
        jnp.where(left > 0, base, -400.0),
    ]
    for i, coef in enumerate(coefs):
        coef_ref[:, i, :] = coef
    coef_ref[:, 6, :] = jnp.zeros_like(a)
    coef_ref[:, 7, :] = jnp.zeros_like(a)

    def shade(g, _):
        several = [unrolls[1] * g + i for i in range(unrolls[1])]
        blank, pad = jnp.zeros((8, K), BF16), jnp.zeros((4, K), F32)
        exponents = [
            dot_nn(pixel_columns, jnp.concatenate([*split3(coef_ref[t]), blank], 0))
            for t in several
        ]
        slopes, cot_rows = [], []
        for t in several:
            cot_high, cot_low = split2(cot_ref[t])
            ch, cl = cot_high.astype(F32), cot_low.astype(F32)
            cot_columns = jnp.concatenate([ch, ch, cl, cl, pad], 0).T.astype(BF16)
            colors = jnp.concatenate([entry_ref[c, pl.ds(t, 1), :] for c in range(5, 8)], 0)
            color_high, color_low = split2(colors)
            kh, kl = color_high.astype(F32), color_low.astype(F32)
            color_rows = jnp.concatenate([kh, kl, kh, kl, pad], 0).astype(BF16)
            slopes.append(dot_nn(cot_columns, color_rows))
            cot_rows.append(jnp.concatenate([ch, cl, pad[0:2]], 0).astype(BF16))
        alphas = [jnp.exp2(exponent) for exponent in exponents]
        log_keeps = [jnp.log(1.0 - alpha) for alpha in alphas]
        prefixes = [
            dot_nn(jnp.concatenate(split2(log_keep), 1), dots_ref[0 : 2 * K])
            for log_keep in log_keeps
        ]
        weights = [jnp.exp(prefix) * alpha for prefix, alpha in zip(prefixes, alphas)]
        pulls = [weight * slope for weight, slope in zip(weights, slopes)]
        suffixes = [
            dot_nn(jnp.concatenate(split2(pull), 1), dots_ref[2 * K : 4 * K]) for pull in pulls
        ]
        for t, weight, rows in zip(several, weights, cot_rows):
            both = jnp.concatenate(split2(weight), 0)
            sums_ref[t, 8:16, :] = dot_nn(jnp.concatenate([rows, rows], 1), both)
        mass = jnp.concatenate([monomials, monomials], 1)
        for t, alpha, log_keep, pull, suffix in zip(several, alphas, log_keeps, pulls, suffixes):
            q = pull - alpha * jnp.exp(-log_keep) * suffix
            sums_ref[t, 0:8, :] = dot_nn(mass, jnp.concatenate(split2(q), 0))
        return 0

    lax.fori_loop(0, tiles // unrolls[1], shade, 0)
    mxx, mxy, myy, mx, my, m0 = [sums_ref[:, i, :] for i in range(6)]
    sx, sy = mx - cx * m0, my - cy * m0
    entry_ref[0] = a * sx + b * sy
    entry_ref[1] = b * sx + c2 * sy
    entry_ref[2] = -0.5 * (mxx - cx * (mx + sx))
    entry_ref[3] = -(mxy - cx * my - cy * sx)
    entry_ref[4] = -0.5 * (myy - cy * (my + sy))
    for i in range(3):
        entry_ref[5 + i] = sums_ref[:, 8 + i, :] + sums_ref[:, 11 + i, :]
    entry_ref[8] = (1.0 - opacity) * m0

    def give(g, _):
        sides, hots = [], []
        for i in range(unrolls[2]):
            t = unrolls[2] * g + i
            hot = hot16(LANES, rank_ref[pl.ds(t, 1), :])
            hits = hits16(owners, owner_row(t))
            placed = []
            for c in range(9):
                high, low = split2(entry_ref[c, pl.ds(t, 1), :])
                placed.append(jnp.concatenate([keep16(hits, high), keep16(hits, low)], 1))
            sides.append(jnp.concatenate(placed, 0))
            hots += [hot, hot]
        grad_ref[...] += dot_nt(jnp.concatenate(sides, 1), jnp.concatenate(hots, 1))
        return 0

    lax.fori_loop(0, tiles // unrolls[2], give, 0)
    for c in range(9):
        out_ref[pl.ds(c, owners, stride=9), :] = grad_ref[c * owners : (c + 1) * owners, :]


def collect_kernel(place_ref, vals_ref, geo_ref, look_ref):
    owners = geo_ref.shape[0]
    total = place_ref[0, owners - 1] + place_ref[0, 2 * owners - 1]
    blank = jnp.zeros((16, LANES), F32)

    def store(at, block):
        geo_ref[pl.ds(at, 1), 0:5, :] = block[None, 0:5]
        look_ref[pl.ds(at, 1), :, :] = block[None, 5:9]

    def compact(g, now):
        values = vals_ref[pl.ds(pl.multiple_of(g * 72, 8), 72), :]
        for j in range(8):
            s = g * 8 + j
            offset = place_ref[0, s]
            following = offset + place_ref[0, owners + s]
            row = jnp.concatenate([values[9 * j : 9 * j + 9], blank[0:7]], 0)
            rolled = pltpu.roll(row, offset & 127, 1)
            block, now = merge(now, rolled, offset, following)
            store(offset >> 7, block)
        return now

    now = lax.fori_loop(0, owners // 8, compact, blank)

    @pl.when(total < owners * LANES)
    def _():
        store(total >> 7, now)

    for more in range(1, WIDE):

        @pl.when(total + more * LANES < owners * LANES)
        def _():
            store((total >> 7) + more, blank)


def add_chunks(ids_ref, value_refs, total, acc_ref, transposed=False):
    def chunk(j, _):
        sides, hots = [], []
        for at in range(0, WIDE, 2):
            first = WIDE * j + at
            ids = ids_row(ids_ref, first)
            hot = hot_rows(ids)
            hits = hits16(LOW, ids & (LOW - 1))
            stacked = []
            for ref, number in value_refs:
                for c in range(number):
                    row = jnp.concatenate(
                        [ref[first, c : c + 1, :], ref[first + 1, c : c + 1, :]], 1
                    )
                    high, low = split2(row)
                    stacked.append(
                        jnp.concatenate([keep16(hits, high), keep16(hits, low)], 1)
                    )
            sides.append(jnp.concatenate(stacked, 0))
            hots += [hot, hot]
        side, hot = jnp.concatenate(sides, 1), jnp.concatenate(hots, 1)
        if transposed:
            acc_ref[...] += dot_nt(hot, side)
        else:
            acc_ref[...] += dot_nt(side, hot)
        return 0

    lax.fori_loop(0, chunks_of(total), chunk, 0)


def spread_out(part):
    return jnp.concatenate([part[:, :256], part[:, 256:]], 0).T


def scatter_kernel(place_ref, ids_ref, geo_vals_ref, look_vals_ref, geo_ref, look_acc_ref, acc_ref):
    owners = geo_vals_ref.shape[0]
    total = place_ref[0, owners - 1] + place_ref[0, 2 * owners - 1]
    acc_ref[...] = jnp.zeros_like(acc_ref)
    add_chunks(ids_ref, [(geo_vals_ref, 5), (look_vals_ref, 4)], total, acc_ref)
    for c in range(5):
        geo_ref[c] = spread_out(acc_ref[c * LOW : (c + 1) * LOW, :])
    look_acc_ref[...] = acc_ref[5 * LOW :, :]


def finish_kernel(*refs):
    others = (len(refs) - 5) // 2
    ids_refs, vals_refs = refs[:others], refs[others : 2 * others]
    start_ref, look_ref, acc_ref, place_ref, sem = refs[2 * others :]
    owners = vals_refs[0].shape[0]
    copies = [
        pltpu.make_async_copy(ref.at[pl.ds(owners, 8), :], place_ref.at[i], sem.at[i])
        for i, ref in enumerate(ids_refs)
    ]
    for copy in copies:
        copy.start()
    acc_ref[...] = start_ref[...].T
    for copy in copies:
        copy.wait()
    for i in range(others):
        total = place_ref[i, 0, owners - 1] + place_ref[i, 0, 2 * owners - 1]
        add_chunks(ids_refs[i], [(vals_refs[i], 4)], total, acc_ref, transposed=True)
    for c in range(4):
        part = acc_ref[:, c * LOW : (c + 1) * LOW]
        look_ref[:, c, :] = jnp.concatenate([part[:256], part[256:]], 1)


VMEM = pl.BlockSpec(memory_space=pltpu.VMEM)
SMEM = pl.BlockSpec(memory_space=pltpu.SMEM)
LIMIT = pltpu.CompilerParams(vmem_limit_bytes=40 * 1024 * 1024)


def exchange(values, owners, axis="owner"):
    sent = values.reshape(owners, 1, -1)
    got = lax.all_to_all(sent, axis, split_axis=0, concat_axis=0, tiled=True)
    return got.reshape(values.shape)


def shards(geometry, appearance, list_owner, list_local, counts, cotangent):
    owners = lax.axis_size("owner")
    views = lax.axis_size("view")
    tiles = counts.shape[1]
    gauss = geometry.shape[2]
    rows = gauss // LANES
    target = list_owner.reshape(1, tiles * K)
    requests, ranks = pl.pallas_call(
        plan_kernel,
        out_shape=(
            jax.ShapeDtypeStruct((owners, LANES), jnp.int32),
            jax.ShapeDtypeStruct((tiles, K), jnp.int32),
        ),
        in_specs=[SMEM, VMEM, VMEM],
        out_specs=(VMEM, VMEM),
        compiler_params=LIMIT,
    )(counts, target, list_local)
    table = pl.pallas_call(
        table_kernel,
        out_shape=jax.ShapeDtypeStruct((9 * LOW, 1024), BF16),
        in_specs=[VMEM, VMEM],
        out_specs=VMEM,
        compiler_params=LIMIT,
    )(geometry.reshape(5, rows, LANES), appearance.reshape(4, rows, LANES))
    asked = exchange(requests, owners)
    picked, packed = pl.pallas_call(
        gather_kernel,
        out_shape=(
            jax.ShapeDtypeStruct((owners * 9, LANES), F32),
            jax.ShapeDtypeStruct((owners + 8, LANES), jnp.int32),
        ),
        in_specs=[VMEM, VMEM],
        out_specs=(VMEM, VMEM),
        scratch_shapes=[
            pltpu.SMEM((8, LANES), jnp.int32),
            pltpu.VMEM((owners + WIDE, 16, LANES), F32),
            pltpu.SemaphoreType.DMA,
        ],
        compiler_params=LIMIT,
    )(asked, table)
    fetched = exchange(picked, owners)
    shifts = [[(i, (i + k) % views) for i in range(views)] for k in range(1, views)]
    other_ids = [lax.ppermute(packed, "view", shift) for shift in shifts]
    fetched, other_ids = lax.optimization_barrier((fetched, other_ids))
    outgoing = pl.pallas_call(
        functools.partial(tile_kernel, (8, 4, 8)),
        out_shape=jax.ShapeDtypeStruct((owners * 9, LANES), F32),
        in_specs=[SMEM, VMEM, VMEM, VMEM, VMEM],
        out_specs=VMEM,
        scratch_shapes=[
            pltpu.VMEM((9 * owners, 2 * LANES), BF16),
            pltpu.VMEM((9 * owners, LANES), F32),
            pltpu.VMEM((4 * K, K), BF16),
            pltpu.VMEM((9, tiles, K), F32),
            pltpu.VMEM((tiles, 8, K), F32),
            pltpu.VMEM((tiles, 16, K), F32),
        ],
        compiler_params=LIMIT,
    )(counts, target, ranks, cotangent[0], fetched)
    returned = exchange(outgoing, owners)
    place = packed[owners:]
    geo_vals, look_vals = pl.pallas_call(
        collect_kernel,
        out_shape=(
            jax.ShapeDtypeStruct((owners, 8, LANES), F32),
            jax.ShapeDtypeStruct((owners, 4, LANES), F32),
        ),
        in_specs=[SMEM, VMEM],
        out_specs=(VMEM, VMEM),
        compiler_params=LIMIT,
    )(place, returned)
    other_vals = [lax.ppermute(look_vals, "view", shift) for shift in shifts]
    geo, look_acc = pl.pallas_call(
        scatter_kernel,
        out_shape=(
            jax.ShapeDtypeStruct((5, rows, LANES), F32),
            jax.ShapeDtypeStruct((4 * LOW, 512), F32),
        ),
        in_specs=[SMEM, VMEM, VMEM, VMEM],
        out_specs=(VMEM, VMEM),
        scratch_shapes=[pltpu.VMEM((9 * LOW, 512), F32)],
        compiler_params=LIMIT,
    )(place, packed, geo_vals, look_vals)
    look = pl.pallas_call(
        finish_kernel,
        out_shape=jax.ShapeDtypeStruct((rows, 4, LANES), F32),
        in_specs=[VMEM] * (2 * views - 1),
        out_specs=VMEM,
        scratch_shapes=[
            pltpu.VMEM((512, 4 * LOW), F32),
            pltpu.SMEM((views - 1, 8, LANES), jnp.int32),
            pltpu.SemaphoreType.DMA((views - 1,)),
        ],
        compiler_params=LIMIT,
    )(*other_ids, *other_vals, look_acc)
    look = jnp.transpose(look, (1, 0, 2)).reshape(4, gauss)
    return (geo.reshape(1, 5, gauss), look)


def solution(mesh):
    placed = (
        P("view", None, "owner"),
        P(None, "owner"),
        P("view", "owner", None),
        P("view", "owner"),
        P("view", "owner"),
        P("view", "owner", None, None),
    )
    return jax.shard_map(
        shards,
        mesh=mesh,
        in_specs=placed,
        out_specs=(P("view", None, "owner"), P(None, "owner")),
        check_vma=False,
    )
```

```python
import functools
import math

import jax
import jax.numpy as jnp
from jax import lax
from jax.experimental import pallas as pl
from jax.experimental.pallas import tpu as pltpu
from jax.sharding import PartitionSpec as P

K = 256
TS = 16
LANES = 128
LOW = 64
F32 = jnp.float32
BF16 = jnp.bfloat16
LOG2E = 1.4426950408889634


def split2(x):
    high = x.astype(BF16)
    return high, (x - high.astype(F32)).astype(BF16)


def split3(x):
    high = x.astype(BF16)
    rest = x - high.astype(F32)
    middle = rest.astype(BF16)
    return high, middle, (rest - middle.astype(F32)).astype(BF16)


def dot_nn(a, b):
    return lax.dot_general(a, b, (((1,), (0,)), ((), ())), preferred_element_type=F32)


def dot_nt(a, b):
    return lax.dot_general(a, b, (((1,), (1,)), ((), ())), preferred_element_type=F32)


def row_iota(rows, columns):
    return lax.broadcasted_iota(jnp.int32, (rows, columns), 0)


def lane_iota(rows, columns):
    return lax.broadcasted_iota(jnp.int32, (rows, columns), 1)


def named_mask(owner_row, count, owners):
    live = lane_iota(1, K) < count
    shown = jnp.where(live, owner_row, -1)
    return row_iota(owners, K) == shown


def plan_kernel(counts_ref, owner_hbm, local_hbm, request_ref, rank_ref, owner_ref, local_ref, sem):
    copies = [
        pltpu.make_async_copy(owner_hbm, owner_ref, sem.at[0]),
        pltpu.make_async_copy(local_hbm, local_ref, sem.at[1]),
    ]
    for copy in copies:
        copy.start()
    tiles = rank_ref.shape[0]
    owners = request_ref.shape[0]
    before = (row_iota(K, K) < lane_iota(K, K)).astype(BF16)
    for copy in copies:
        copy.wait()
    rows = [owner_ref[:, t * K : (t + 1) * K] for t in range(tiles)]
    rows = [
        jnp.where(lane_iota(1, K) < counts_ref[0, t], row, -1) for t, row in enumerate(rows)
    ]
    ids = [local_ref[:, t * K : (t + 1) * K] for t in range(tiles)]
    units = [jnp.where((i & LOW) != 0, 256.0, 1.0) for i in ids]
    found = [hits16(owners, row) for row in rows]
    halves = [keep16(f, jnp.ones((owners, K), BF16)) for f in found]
    scaled = [keep16(f, unit.astype(BF16)) for f, unit in zip(found, units)]
    inside = dot_nn(jnp.concatenate(scaled, 0), before)
    carry = jnp.zeros((owners, 1), F32)
    sides = []
    for t, row in enumerate(rows):
        named = row_iota(owners, K) == row
        here = inside[t * owners : (t + 1) * owners]
        both = jnp.sum(jnp.where(named, here + carry, 0.0), axis=0, keepdims=True)
        both = both.astype(jnp.int32)
        rank = jnp.where((ids[t] & LOW) != 0, LANES - 1 - (both >> 8), both & 255)
        carry = carry + jnp.sum(jnp.where(named, units[t], 0.0), axis=1, keepdims=True)
        rank_ref[t : t + 1, :] = rank
        asked = ids[t] + 1
        hits = hits16(LANES, rank)
        high = keep16(hits, (asked >> 7).astype(F32).astype(BF16))
        low = keep16(hits, (asked & 127).astype(F32).astype(BF16))
        sides.append(jnp.concatenate([high, low], 0))
    total = dot_nt(jnp.concatenate(halves, 1), jnp.concatenate(sides, 1))
    request_ref[...] = (total[:, :LANES] * 128.0 + total[:, LANES:]).astype(jnp.int32)


def table_kernel(geo_ref, app_ref, table_ref):
    for c in range(9):
        values = geo_ref[c] if c < 5 else app_ref[c - 5]
        high, low = split2(values.T)
        for bucket in range(2):
            at = slice(bucket * LOW, (bucket + 1) * LOW)
            table_ref[bucket, c * LOW : (c + 1) * LOW, :] = jnp.concatenate(
                [high[at], low[at]], 1
            )


WIDE = 8
NARROW = 4


def ids_row(ref, at):
    return jnp.concatenate([ref[pl.ds(at, 1), :], ref[pl.ds(at + 1, 1), :]], 1) - 1


def hits16(rows, row):
    return lax.broadcasted_iota(jnp.int16, (rows, row.shape[1]), 0) == row.astype(jnp.int16)


def keep16(hits, row):
    return jnp.where(hits, row, jnp.zeros_like(row))


def hot16(rows, row):
    return keep16(hits16(rows, row), jnp.ones((rows, row.shape[1]), BF16))


def hot_rows(ids, bucket):
    fits = (ids >= 0) & (((ids >> 6) & 1) == bucket)
    return hot16(256, jnp.where(fits, ids >> 7, -1))


def low_mask(ids):
    return row_iota(LOW, 256) == (ids & (LOW - 1))


def each_chunk(totals, owners, chunk):
    most = jnp.maximum(totals[0], totals[1])
    large = most // (WIDE * LANES)
    small = (most - large * (WIDE * LANES) + NARROW * LANES - 1) // (NARROW * LANES)

    def wide(j, _):
        chunk(WIDE * j, 0, WIDE)
        chunk(owners - WIDE * (j + 1), 1, WIDE)
        return 0

    def narrow(j, _):
        done = WIDE * large + NARROW * j
        chunk(done, 0, NARROW)
        chunk(owners - done - NARROW, 1, NARROW)
        return 0

    lax.fori_loop(0, large, wide, 0)
    lax.fori_loop(0, small, narrow, 0)


def compact(owners, ends_ref, bucket, start, row_at, load, store):
    lanes = lane_iota(*row_at(0, 0).shape)

    def group(g, carry):
        offset, now = carry
        for j in range(8):
            s = g * 8 + j
            end = start + ends_ref[0, bucket * owners + s]
            amount = end - offset
            row = row_at(g, j)
            if bucket == 0:
                row = jnp.where(lanes < amount, row, jnp.zeros_like(row))
                rolled = pltpu.roll(row, offset & 127, 1)
            else:
                row = jnp.where(lanes >= LANES - amount, row, jnp.zeros_like(row))
                rolled = pltpu.roll(row, end & 127, 1)
            fits = lanes >= (offset & 127)
            block = now + jnp.where(fits, rolled, jnp.zeros_like(rolled))
            spilt = jnp.where(fits, jnp.zeros_like(rolled), rolled)
            store(offset >> 7, block)
            now = jnp.where((end >> 7) > (offset >> 7), spilt, block)
            offset = end
        return offset, now

    offset, now = lax.fori_loop(0, owners // 8, group, (start, load(start >> 7)))
    store(offset >> 7, now)


def gather_kernel(asked_ref, table_ref, out_ref, packed_ref, ends_ref, found_ref):
    owners = asked_ref.shape[0]
    asked = asked_ref[...]
    odd = ((asked - 1) & LOW) != 0
    valid = [(asked > 0) & ~odd, (asked > 0) & odd]
    valid = jnp.concatenate([v.astype(F32).astype(BF16) for v in valid], 1)
    upto = (row_iota(owners, owners) >= lane_iota(owners, owners)).astype(F32).astype(BF16)
    sides = ((lane_iota(8, 2 * LANES) >> 7) == row_iota(8, 2 * LANES)).astype(F32).astype(BF16)
    ends = dot_nt(sides, dot_nn(upto, valid).astype(BF16)).astype(jnp.int32)
    packed_ref[...] = jnp.zeros_like(packed_ref)
    for s in range(owners):
        ends_ref[0, s] = ends[0, s]
        ends_ref[0, owners + s] = ends[1, s]
    totals = ends[0, owners - 1], ends[1, owners - 1]
    base = owners * LANES - totals[1]

    def row_at(g, j):
        return jnp.broadcast_to(asked_ref[pl.ds(g * 8 + j, 1), :], (8, LANES))

    def load(at):
        return jnp.broadcast_to(packed_ref[pl.ds(at, 1), :], (8, LANES))

    def store(at, block):
        packed_ref[pl.ds(at, 1), :] = block[0:1]

    for bucket in range(2):
        compact(owners, ends_ref, bucket, base if bucket else 0, row_at, load, store)
    packed_ref[owners + 1 : owners + 2, 0 : 2 * owners] = jnp.concatenate(
        [ends[0:1], ends[1:2]], 1
    )

    def chunk(row, bucket, wide):
        for at in range(0, wide, 2):
            ids = ids_row(packed_ref, row + at)
            hot = hot_rows(ids, bucket)
            found = dot_nn(table_ref[bucket], jnp.concatenate([hot, hot], 0))
            mask = low_mask(ids)
            rows = [
                jnp.sum(jnp.where(mask, found[c * LOW : (c + 1) * LOW], 0.0), axis=0, keepdims=True)
                for c in range(9)
            ]
            values = jnp.concatenate(rows, 0)
            found_ref[bucket, row + at + 1, 0:9, :] = values[:, :LANES]
            found_ref[bucket, row + at + 2, 0:9, :] = values[:, LANES:]

    each_chunk(totals, owners, chunk)

    def expand(g, offsets):
        lanes = lane_iota(16, LANES)
        low, high = offsets
        blocks = []
        for j in range(8):
            s = g * 8 + j
            low_end, high_end = ends_ref[0, s], base + ends_ref[0, owners + s]
            sources = []
            for bucket, at, row in ((0, low, (low >> 7) + 1), (1, high_end, high_end >> 7)):
                back = (LANES - (at & 127)) & 127
                first = pltpu.roll(found_ref[bucket, row], back, 1)
                second = pltpu.roll(found_ref[bucket, row + 1], back, 1)
                sources.append(jnp.where(lanes + (at & 127) < LANES, first, second))
            values = jnp.where(lanes >= LANES - (high_end - high), sources[1], 0.0)
            values = jnp.where(lanes < low_end - low, sources[0], values)
            blocks.append(values[0:9])
            low, high = low_end, high_end
        out_ref[pl.ds(pl.multiple_of(g * 72, 8), 72), :] = jnp.concatenate(blocks, 0)
        return low, high

    lax.fori_loop(0, owners // 8, expand, (0, base))


def pixel_rows():
    pixel = lane_iota(1, K)
    u = ((pixel & (TS - 1)).astype(F32) + 0.5) / TS - 0.5
    v = ((pixel >> 4).astype(F32) + 0.5) / TS - 0.5
    one = jnp.ones((1, K), F32)
    zero = jnp.zeros((2, K), F32)
    return jnp.concatenate([u * u, u * v, v * v, u, v, one, zero], 0)


def tile_kernel(
    unrolls,
    counts_ref,
    owner_ref,
    rank_ref,
    cot_ref,
    fetched_ref,
    out_ref,
    table_ref,
    grad_ref,
    dots_ref,
    entry_ref,
    coef_ref,
    sums_ref,
):
    tiles = rank_ref.shape[0]
    owners = fetched_ref.shape[0] // 9
    unrolls = [math.gcd(tiles, n) for n in unrolls]
    half = owners // 2
    for c in range(9):
        even = fetched_ref[pl.ds(c, half, stride=18), :]
        odd = fetched_ref[pl.ds(9 + c, half, stride=18), :]
        high, low = split2(jnp.concatenate([even, odd], 1))
        table_ref[c * half : (c + 1) * half, :] = jnp.concatenate([high, low], 1)
    grad_ref[...] = jnp.zeros_like(grad_ref)
    pixels = pixel_rows()
    monomials = pixels.astype(BF16)
    pixel_columns = jnp.concatenate([pixels] * 4, 0).T.astype(BF16)
    before = (row_iota(K, K) < lane_iota(K, K)).astype(BF16)
    after = (row_iota(K, K) > lane_iota(K, K)).astype(BF16)
    dots_ref[0:K] = before
    dots_ref[K : 2 * K] = after

    def owner_row(t):
        row = owner_ref[:, pl.ds(pl.multiple_of(t * K, K), K)]
        return jnp.where(lane_iota(1, K) < counts_ref[0, t], row, -1)

    def hot_place(t):
        row = owner_row(t)
        return hot16(2 * LANES, rank_ref[pl.ds(t, 1), :] + (row & 1) * LANES)

    def fetch(g, _):
        several = [unrolls[0] * g + i for i in range(unrolls[0])]
        hots = [hot_place(t) for t in several]
        spreads = [dot_nn(table_ref[...], jnp.concatenate([hot, hot], 0)) for hot in hots]
        for t, spread in zip(several, spreads):
            named = row_iota(half, K) == (owner_row(t) >> 1)
            for c in range(9):
                kept = jnp.where(named, spread[c * half : (c + 1) * half], 0.0)
                entry_ref[c, pl.ds(t, 1), :] = jnp.sum(kept, axis=0, keepdims=True)
        return 0

    lax.fori_loop(0, tiles // unrolls[0], fetch, 0)
    cx, cy = entry_ref[0] - 0.5, entry_ref[1] - 0.5
    a, b, c2 = entry_ref[2], entry_ref[3], entry_ref[4]
    opacity = 1.0 / (1.0 + jnp.exp(-entry_ref[8]))
    spots = lane_iota(1, K)
    left = jnp.concatenate([counts_ref[0, t] - spots for t in range(tiles)], 0)
    ax, ay = a * cx + b * cy, b * cx + c2 * cy
    base = jnp.log(0.99 * opacity) * LOG2E - (0.5 * LOG2E) * (ax * cx + ay * cy)
    coefs = [
        (-0.5 * LOG2E) * a,
        -LOG2E * b,
        (-0.5 * LOG2E) * c2,
        LOG2E * ax,
        LOG2E * ay,
        jnp.where(left > 0, base, -400.0),
    ]
    for i, coef in enumerate(coefs):
        coef_ref[:, i, :] = coef
    coef_ref[:, 6, :] = jnp.zeros_like(a)
    coef_ref[:, 7, :] = jnp.zeros_like(a)

    def scans(arrays, triangle):
        parts = [part for array in arrays for part in split2(array)]
        done = dot_nn(jnp.concatenate(parts, 0), triangle)
        pieces = [done[i * K : (i + 1) * K] for i in range(len(parts))]
        return [high + low for high, low in zip(pieces[0::2], pieces[1::2])]

    def shade(g, _):
        several = [unrolls[1] * g + i for i in range(unrolls[1])]
        blank, pad = jnp.zeros((8, K), BF16), jnp.zeros((4, K), F32)
        exponents = [
            dot_nn(pixel_columns, jnp.concatenate([*split3(coef_ref[t]), blank], 0))
            for t in several
        ]
        slopes, cot_rows = [], []
        for t in several:
            cot_high, cot_low = split2(cot_ref[t])
            ch, cl = cot_high.astype(F32), cot_low.astype(F32)
            cot_columns = jnp.concatenate([ch, ch, cl, cl, pad], 0).T.astype(BF16)
            colors = jnp.concatenate([entry_ref[c, pl.ds(t, 1), :] for c in range(5, 8)], 0)
            color_high, color_low = split2(colors)
            kh, kl = color_high.astype(F32), color_low.astype(F32)
            color_rows = jnp.concatenate([kh, kl, kh, kl, pad], 0).astype(BF16)
            slopes.append(dot_nn(cot_columns, color_rows))
            cot_rows.append(jnp.concatenate([ch, cl, pad[0:2]], 0).astype(BF16))
        alphas = [jnp.exp2(exponent) for exponent in exponents]
        log_keeps = [jnp.log(1.0 - alpha) for alpha in alphas]
        prefixes = scans(log_keeps, dots_ref[0:K])
        weights = [jnp.exp(prefix) * alpha for prefix, alpha in zip(prefixes, alphas)]
        pulls = [weight * slope for weight, slope in zip(weights, slopes)]
        suffixes = scans(pulls, dots_ref[K : 2 * K])
        for t, weight, rows in zip(several, weights, cot_rows):
            both = jnp.concatenate(split2(weight), 0)
            sums_ref[t, 8:16, :] = dot_nn(jnp.concatenate([rows, rows], 1), both)
        mass = jnp.concatenate([monomials, monomials], 1)
        for t, alpha, log_keep, pull, suffix in zip(several, alphas, log_keeps, pulls, suffixes):
            q = pull - alpha * jnp.exp(-log_keep) * suffix
            sums_ref[t, 0:8, :] = dot_nn(mass, jnp.concatenate(split2(q), 0))
        return 0

    lax.fori_loop(0, tiles // unrolls[1], shade, 0)
    mxx, mxy, myy, mx, my, m0 = [sums_ref[:, i, :] for i in range(6)]
    sx, sy = mx - cx * m0, my - cy * m0
    entry_ref[0] = a * sx + b * sy
    entry_ref[1] = b * sx + c2 * sy
    entry_ref[2] = -0.5 * (mxx - cx * (mx + sx))
    entry_ref[3] = -(mxy - cx * my - cy * sx)
    entry_ref[4] = -0.5 * (myy - cy * (my + sy))
    for i in range(3):
        entry_ref[5 + i] = sums_ref[:, 8 + i, :] + sums_ref[:, 11 + i, :]
    entry_ref[8] = (1.0 - opacity) * m0

    def give(g, _):
        sides, hots = [], []
        for i in range(unrolls[2]):
            t = unrolls[2] * g + i
            hot = hot_place(t)
            hits = hits16(half, owner_row(t) >> 1)
            placed = []
            for c in range(9):
                high, low = split2(entry_ref[c, pl.ds(t, 1), :])
                placed.append(jnp.concatenate([keep16(hits, high), keep16(hits, low)], 1))
            sides.append(jnp.concatenate(placed, 0))
            hots += [hot, hot]
        grad_ref[...] += dot_nt(jnp.concatenate(sides, 1), jnp.concatenate(hots, 1))
        return 0

    lax.fori_loop(0, tiles // unrolls[2], give, 0)
    for c in range(9):
        part = grad_ref[c * half : (c + 1) * half, :]
        out_ref[pl.ds(c, half, stride=18), :] = part[:, :LANES]
        out_ref[pl.ds(9 + c, half, stride=18), :] = part[:, LANES:]


def collect_kernel(ends_ref, vals_ref, geo_ref, look_ref):
    owners = vals_ref.shape[0] // 9
    base = owners * LANES - ends_ref[0, 2 * owners - 1]
    geo_ref[...] = jnp.zeros_like(geo_ref)
    look_ref[...] = jnp.zeros_like(look_ref)
    blank = jnp.zeros((7, LANES), F32)

    def row_at(g, j):
        rows = vals_ref[pl.ds(pl.multiple_of(g * 72, 8), 72), :]
        return jnp.concatenate([rows[9 * j : 9 * j + 9], blank], 0)

    def load(at):
        return jnp.concatenate([geo_ref[at, 0:5], look_ref[at], blank], 0)

    def store(at, block):
        geo_ref[pl.ds(at, 1), 0:5, :] = block[None, 0:5]
        look_ref[pl.ds(at, 1), :, :] = block[None, 5:9]

    for bucket in range(2):
        compact(owners, ends_ref, bucket, base if bucket else 0, row_at, load, store)


def add_chunks(ids_ref, value_refs, totals, owners, acc_ref, transposed=False):
    def chunk(row, bucket, wide):
        sides, hots = [], []
        for at in range(0, wide, 2):
            first = row + at
            ids = ids_row(ids_ref, first)
            hot = hot_rows(ids, bucket)
            hits = hits16(LOW, ids & (LOW - 1))
            stacked = []
            for ref, number in value_refs:
                for c in range(number):
                    pair = jnp.concatenate(
                        [ref[first, c : c + 1, :], ref[first + 1, c : c + 1, :]], 1
                    )
                    high, low = split2(pair)
                    stacked.append(
                        jnp.concatenate([keep16(hits, high), keep16(hits, low)], 1)
                    )
            sides.append(jnp.concatenate(stacked, 0))
            hots += [hot, hot]
        side, hot = jnp.concatenate(sides, 1), jnp.concatenate(hots, 1)
        if transposed:
            acc_ref[bucket] += dot_nt(hot, side)
        else:
            acc_ref[bucket] += dot_nt(side, hot)

    each_chunk(totals, owners, chunk)


def scatter_kernel(ends_ref, ids_ref, geo_vals_ref, look_vals_ref, geo_ref, look_acc_ref, acc_ref):
    owners = geo_vals_ref.shape[0] - 1
    totals = ends_ref[0, owners - 1], ends_ref[0, 2 * owners - 1]
    acc_ref[...] = jnp.zeros_like(acc_ref)
    add_chunks(ids_ref, [(geo_vals_ref, 5), (look_vals_ref, 4)], totals, owners, acc_ref)
    for c in range(5):
        at = slice(c * LOW, (c + 1) * LOW)
        geo_ref[c] = jnp.concatenate([acc_ref[0, at], acc_ref[1, at]], 0).T
    look_acc_ref[...] = acc_ref[:, 5 * LOW :, :]


def finish_kernel(*refs):
    others = (len(refs) - 3) // 2
    ids_refs, vals_refs = refs[:others], refs[others : 2 * others]
    start_ref, look_ref, acc_ref = refs[2 * others :]
    owners = vals_refs[0].shape[0] - 1
    places = [ref[owners + 1 : owners + 2, :] for ref in ids_refs]
    totals = [(place[0, owners - 1], place[0, 2 * owners - 1]) for place in places]
    for bucket in range(2):
        acc_ref[bucket] = start_ref[bucket].T
    for i, ends in enumerate(totals):
        add_chunks(ids_refs[i], [(vals_refs[i], 4)], ends, owners, acc_ref, transposed=True)
    for c in range(4):
        at = slice(c * LOW, (c + 1) * LOW)
        look_ref[:, c, :] = jnp.concatenate([acc_ref[0, :, at], acc_ref[1, :, at]], 1)


HBM = pl.BlockSpec(memory_space=pltpu.HBM)
VMEM = pl.BlockSpec(memory_space=pltpu.VMEM)
SMEM = pl.BlockSpec(memory_space=pltpu.SMEM)
LIMIT = pltpu.CompilerParams(vmem_limit_bytes=40 * 1024 * 1024)


def exchange(values, owners, axis="owner"):
    sent = values.reshape(owners, 1, -1)
    got = lax.all_to_all(sent, axis, split_axis=0, concat_axis=0, tiled=True)
    return got.reshape(values.shape)


def shards(geometry, appearance, list_owner, list_local, counts, cotangent):
    owners = lax.axis_size("owner")
    views = lax.axis_size("view")
    tiles = counts.shape[1]
    gauss = geometry.shape[2]
    rows = gauss // LANES
    target = list_owner.reshape(1, tiles * K)
    requests, ranks = pl.pallas_call(
        plan_kernel,
        out_shape=(
            jax.ShapeDtypeStruct((owners, LANES), jnp.int32),
            jax.ShapeDtypeStruct((tiles, K), jnp.int32),
        ),
        in_specs=[SMEM, HBM, HBM],
        out_specs=(VMEM, VMEM),
        scratch_shapes=[
            pltpu.VMEM((1, tiles * K), jnp.int32),
            pltpu.VMEM((1, tiles * K), jnp.int32),
            pltpu.SemaphoreType.DMA((2,)),
        ],
        compiler_params=pltpu.CompilerParams(vmem_limit_bytes=60 * 1024 * 1024),
    )(counts, target, list_local)
    table = pl.pallas_call(
        table_kernel,
        out_shape=jax.ShapeDtypeStruct((2, 9 * LOW, 512), BF16),
        in_specs=[VMEM, VMEM],
        out_specs=VMEM,
        compiler_params=LIMIT,
    )(geometry.reshape(5, rows, LANES), appearance.reshape(4, rows, LANES))
    asked = exchange(requests, owners)
    picked, packed = pl.pallas_call(
        gather_kernel,
        out_shape=(
            jax.ShapeDtypeStruct((owners * 9, LANES), F32),
            jax.ShapeDtypeStruct((owners + 8, LANES), jnp.int32),
        ),
        in_specs=[VMEM, VMEM],
        out_specs=(VMEM, VMEM),
        scratch_shapes=[
            pltpu.SMEM((8, LANES), jnp.int32),
            pltpu.VMEM((2, owners + 2, 16, LANES), F32),
        ],
        compiler_params=LIMIT,
    )(asked, table)
    fetched = exchange(picked, owners)
    shifts = [[(i, (i + k) % views) for i in range(views)] for k in range(1, views)]
    other_ids = [lax.ppermute(packed, "view", shift) for shift in shifts]
    fetched, other_ids = lax.optimization_barrier((fetched, other_ids))
    outgoing = pl.pallas_call(
        functools.partial(tile_kernel, (16, 8, 16)),
        out_shape=jax.ShapeDtypeStruct((owners * 9, LANES), F32),
        in_specs=[SMEM, VMEM, VMEM, VMEM, VMEM],
        out_specs=VMEM,
        scratch_shapes=[
            pltpu.VMEM((9 * owners // 2, 4 * LANES), BF16),
            pltpu.VMEM((9 * owners // 2, 2 * LANES), F32),
            pltpu.VMEM((2 * K, K), BF16),
            pltpu.VMEM((9, tiles, K), F32),
            pltpu.VMEM((tiles, 8, K), F32),
            pltpu.VMEM((tiles, 16, K), F32),
        ],
        compiler_params=LIMIT,
    )(counts, target, ranks, cotangent[0], fetched)
    returned = exchange(outgoing, owners)
    ends = packed[owners + 1 :]
    geo_vals, look_vals = pl.pallas_call(
        collect_kernel,
        out_shape=(
            jax.ShapeDtypeStruct((owners + 1, 8, LANES), F32),
            jax.ShapeDtypeStruct((owners + 1, 4, LANES), F32),
        ),
        in_specs=[SMEM, VMEM],
        out_specs=(VMEM, VMEM),
        compiler_params=LIMIT,
    )(ends, returned)
    other_vals = [lax.ppermute(look_vals, "view", shift) for shift in shifts]
    geo, look_acc = pl.pallas_call(
        scatter_kernel,
        out_shape=(
            jax.ShapeDtypeStruct((5, rows, LANES), F32),
            jax.ShapeDtypeStruct((2, 4 * LOW, 256), F32),
        ),
        in_specs=[SMEM, VMEM, VMEM, VMEM],
        out_specs=(VMEM, VMEM),
        scratch_shapes=[pltpu.VMEM((2, 9 * LOW, 256), F32)],
        compiler_params=LIMIT,
    )(ends, packed, geo_vals, look_vals)
    look = pl.pallas_call(
        finish_kernel,
        out_shape=jax.ShapeDtypeStruct((rows, 4, LANES), F32),
        in_specs=[VMEM] * (2 * views - 1),
        out_specs=VMEM,
        scratch_shapes=[
            pltpu.VMEM((2, 256, 4 * LOW), F32),
        ],
        compiler_params=LIMIT,
    )(*other_ids, *other_vals, look_acc)
    look = jnp.transpose(look, (1, 0, 2)).reshape(4, gauss)
    return (geo.reshape(1, 5, gauss), look)


def solution(mesh):
    placed = (
        P("view", None, "owner"),
        P(None, "owner"),
        P("view", "owner", None),
        P("view", "owner"),
        P("view", "owner"),
        P("view", "owner", None, None),
    )
    return jax.shard_map(
        shards,
        mesh=mesh,
        in_specs=placed,
        out_specs=(P("view", None, "owner"), P(None, "owner")),
        check_vma=False,
    )
```

```python
import functools
import math

import jax
import jax.numpy as jnp
from jax import lax
from jax.experimental import pallas as pl
from jax.experimental.pallas import tpu as pltpu
from jax.sharding import PartitionSpec as P

K = 256
TS = 16
LANES = 128
LOW = 64
F32 = jnp.float32
BF16 = jnp.bfloat16
LOG2E = 1.4426950408889634


def split2(x):
    high = x.astype(BF16)
    return high, (x - high.astype(F32)).astype(BF16)


def split3(x):
    high = x.astype(BF16)
    rest = x - high.astype(F32)
    middle = rest.astype(BF16)
    return high, middle, (rest - middle.astype(F32)).astype(BF16)


def dot_nn(a, b):
    return lax.dot_general(a, b, (((1,), (0,)), ((), ())), preferred_element_type=F32)


def dot_nt(a, b):
    return lax.dot_general(a, b, (((1,), (1,)), ((), ())), preferred_element_type=F32)


def row_iota(rows, columns):
    return lax.broadcasted_iota(jnp.int32, (rows, columns), 0)


def lane_iota(rows, columns):
    return lax.broadcasted_iota(jnp.int32, (rows, columns), 1)


def named_mask(owner_row, count, owners):
    live = lane_iota(1, K) < count
    shown = jnp.where(live, owner_row, -1)
    return row_iota(owners, K) == shown


def plan_kernel(counts_ref, owner_hbm, local_hbm, request_ref, rank_ref, owner_ref, local_ref, sem):
    copies = [
        pltpu.make_async_copy(owner_hbm, owner_ref, sem.at[0]),
        pltpu.make_async_copy(local_hbm, local_ref, sem.at[1]),
    ]
    for copy in copies:
        copy.start()
    tiles = rank_ref.shape[0]
    owners = request_ref.shape[0]
    before = (row_iota(K, K) < lane_iota(K, K)).astype(BF16)
    for copy in copies:
        copy.wait()
    rows = [owner_ref[:, t * K : (t + 1) * K] for t in range(tiles)]
    rows = [
        jnp.where(lane_iota(1, K) < counts_ref[0, t], row, -1) for t, row in enumerate(rows)
    ]
    ids = [local_ref[:, t * K : (t + 1) * K] for t in range(tiles)]
    units = [jnp.where((i & LOW) != 0, 256.0, 1.0) for i in ids]
    found = [hits16(owners, row) for row in rows]
    halves = [keep16(f, jnp.ones((owners, K), BF16)) for f in found]
    scaled = [keep16(f, unit.astype(BF16)) for f, unit in zip(found, units)]
    inside = dot_nn(jnp.concatenate(scaled, 0), before)
    carry = jnp.zeros((owners, 1), F32)
    sides = []
    for t, row in enumerate(rows):
        named = row_iota(owners, K) == row
        here = inside[t * owners : (t + 1) * owners]
        both = jnp.sum(jnp.where(named, here + carry, 0.0), axis=0, keepdims=True)
        both = both.astype(jnp.int32)
        rank = jnp.where((ids[t] & LOW) != 0, LANES - 1 - (both >> 8), both & 255)
        carry = carry + jnp.sum(jnp.where(named, units[t], 0.0), axis=1, keepdims=True)
        rank_ref[t : t + 1, :] = rank
        asked = ids[t] + 1
        hits = hits16(LANES, rank)
        high = keep16(hits, (asked >> 7).astype(F32).astype(BF16))
        low = keep16(hits, (asked & 127).astype(F32).astype(BF16))
        sides.append(jnp.concatenate([high, low], 0))
    total = dot_nt(jnp.concatenate(halves, 1), jnp.concatenate(sides, 1))
    request_ref[...] = (total[:, :LANES] * 128.0 + total[:, LANES:]).astype(jnp.int32)


def table_kernel(geo_ref, app_ref, table_ref):
    for c in range(9):
        values = geo_ref[c] if c < 5 else app_ref[c - 5]
        high, low = split2(values.T)
        for bucket in range(2):
            at = slice(bucket * LOW, (bucket + 1) * LOW)
            table_ref[bucket, c * LOW : (c + 1) * LOW, :] = jnp.concatenate(
                [high[at], low[at]], 1
            )


WIDE = 8
NARROW = 4


def ids_row(ref, at):
    return jnp.concatenate([ref[pl.ds(at, 1), :], ref[pl.ds(at + 1, 1), :]], 1) - 1


def hits16(rows, row):
    return lax.broadcasted_iota(jnp.int16, (rows, row.shape[1]), 0) == row.astype(jnp.int16)


def keep16(hits, row):
    return jnp.where(hits, row, jnp.zeros_like(row))


def hot16(rows, row):
    return keep16(hits16(rows, row), jnp.ones((rows, row.shape[1]), BF16))


def hot_rows(ids, bucket):
    fits = (ids >= 0) & (((ids >> 6) & 1) == bucket)
    return hot16(256, jnp.where(fits, ids >> 7, -1))


def low_mask(ids):
    return row_iota(LOW, 256) == (ids & (LOW - 1))


def each_chunk(totals, owners, chunk):
    most = jnp.maximum(totals[0], totals[1])
    large = most // (WIDE * LANES)
    small = (most - large * (WIDE * LANES) + NARROW * LANES - 1) // (NARROW * LANES)

    def wide(j, _):
        chunk(WIDE * j, 0, WIDE)
        chunk(owners - WIDE * (j + 1), 1, WIDE)
        return 0

    def narrow(j, _):
        done = WIDE * large + NARROW * j
        chunk(done, 0, NARROW)
        chunk(owners - done - NARROW, 1, NARROW)
        return 0

    lax.fori_loop(0, large, wide, 0)
    lax.fori_loop(0, small, narrow, 0)


def compact(owners, ends_ref, base, row_at, store):
    blank = jnp.zeros((8, LANES), row_at(0, 0).dtype)
    lanes = lane_iota(8, LANES)

    def group(g, carry):
        carry = list(carry)
        for j in range(8):
            s = g * 8 + j
            row = row_at(g, j)
            for bucket in range(2):
                offset, now = carry[bucket]
                end = ends_ref[0, bucket * owners + s] + (base if bucket else 0)
                if bucket == 0:
                    part = jnp.where(lanes < end - offset, row, blank)
                    rolled = pltpu.roll(part, offset & 127, 1)
                else:
                    part = jnp.where(lanes >= LANES - (end - offset), row, blank)
                    rolled = pltpu.roll(part, end & 127, 1)
                fits = lanes >= (offset & 127)
                block = now + jnp.where(fits, rolled, blank)
                spilt = jnp.where(fits, blank, rolled)
                store(bucket, offset >> 7, block)
                carry[bucket] = end, jnp.where((end >> 7) > (offset >> 7), spilt, block)
        return tuple(carry)

    carry = lax.fori_loop(0, owners // 8, group, ((0, blank), (base, blank)))
    for bucket, (offset, now) in enumerate(carry):
        store(bucket, offset >> 7, now)


def gather_kernel(asked_ref, table_ref, out_ref, packed_ref, ends_ref, held_ref, found_ref):
    owners = asked_ref.shape[0]
    asked = asked_ref[...]
    odd = ((asked - 1) & LOW) != 0
    valid = [(asked > 0) & ~odd, (asked > 0) & odd]
    valid = jnp.concatenate([v.astype(F32).astype(BF16) for v in valid], 1)
    upto = (row_iota(owners, owners) >= lane_iota(owners, owners)).astype(F32).astype(BF16)
    sides = ((lane_iota(8, 2 * LANES) >> 7) == row_iota(8, 2 * LANES)).astype(F32).astype(BF16)
    ends = dot_nt(sides, dot_nn(upto, valid).astype(BF16)).astype(jnp.int32)
    held_ref[...] = jnp.zeros_like(held_ref)
    for s in range(owners):
        ends_ref[0, s] = ends[0, s]
        ends_ref[0, owners + s] = ends[1, s]
    totals = ends[0, owners - 1], ends[1, owners - 1]
    base = owners * LANES - totals[1]

    def row_at(g, j):
        return jnp.broadcast_to(asked_ref[pl.ds(g * 8 + j, 1), :], (8, LANES))

    def store(bucket, at, block):
        held_ref[bucket, pl.ds(at, 1), :] = block[0:1]

    compact(owners, ends_ref, base, row_at, store)
    packed_ref[...] = held_ref[0] + held_ref[1]
    packed_ref[owners + 1 : owners + 2, 0 : 2 * owners] = jnp.concatenate(
        [ends[0:1], ends[1:2]], 1
    )

    def chunk(row, bucket, wide):
        for at in range(0, wide, 2):
            ids = ids_row(held_ref.at[bucket], row + at)
            hot = hot_rows(ids, bucket)
            found = dot_nn(table_ref[bucket], jnp.concatenate([hot, hot], 0))
            mask = low_mask(ids)
            rows = [
                jnp.sum(jnp.where(mask, found[c * LOW : (c + 1) * LOW], 0.0), axis=0, keepdims=True)
                for c in range(9)
            ]
            values = jnp.concatenate(rows, 0)
            found_ref[bucket, row + at + 1, 0:9, :] = values[:, :LANES]
            found_ref[bucket, row + at + 2, 0:9, :] = values[:, LANES:]

    each_chunk(totals, owners, chunk)

    def expand(g, offsets):
        lanes = lane_iota(16, LANES)
        low, high = offsets
        blocks = []
        for j in range(8):
            s = g * 8 + j
            low_end, high_end = ends_ref[0, s], base + ends_ref[0, owners + s]
            sources = []
            for bucket, at, row in ((0, low, (low >> 7) + 1), (1, high_end, high_end >> 7)):
                back = (LANES - (at & 127)) & 127
                first = pltpu.roll(found_ref[bucket, row], back, 1)
                second = pltpu.roll(found_ref[bucket, row + 1], back, 1)
                sources.append(jnp.where(lanes + (at & 127) < LANES, first, second))
            values = jnp.where(lanes >= LANES - (high_end - high), sources[1], 0.0)
            values = jnp.where(lanes < low_end - low, sources[0], values)
            blocks.append(values[0:9])
            low, high = low_end, high_end
        out_ref[pl.ds(pl.multiple_of(g * 72, 8), 72), :] = jnp.concatenate(blocks, 0)
        return low, high

    lax.fori_loop(0, owners // 8, expand, (0, base))


def pixel_rows():
    pixel = lane_iota(1, K)
    u = ((pixel & (TS - 1)).astype(F32) + 0.5) / TS - 0.5
    v = ((pixel >> 4).astype(F32) + 0.5) / TS - 0.5
    one = jnp.ones((1, K), F32)
    zero = jnp.zeros((2, K), F32)
    return jnp.concatenate([u * u, u * v, v * v, u, v, one, zero], 0)


def tile_kernel(
    unrolls,
    counts_ref,
    owner_ref,
    rank_ref,
    cot_ref,
    fetched_ref,
    out_ref,
    table_ref,
    grad_ref,
    dots_ref,
    entry_ref,
    coef_ref,
    sums_ref,
):
    tiles = rank_ref.shape[0]
    owners = fetched_ref.shape[0] // 9
    unrolls = [math.gcd(tiles, n) for n in unrolls]
    half = owners // 2
    for c in range(9):
        even = fetched_ref[pl.ds(c, half, stride=18), :]
        odd = fetched_ref[pl.ds(9 + c, half, stride=18), :]
        high, low = split2(jnp.concatenate([even, odd], 1))
        table_ref[c * half : (c + 1) * half, :] = jnp.concatenate([high, low], 1)
    grad_ref[...] = jnp.zeros_like(grad_ref)
    pixels = pixel_rows()
    monomials = pixels.astype(BF16)
    pixel_columns = jnp.concatenate([pixels] * 4, 0).T.astype(BF16)
    before = (row_iota(K, K) < lane_iota(K, K)).astype(BF16)
    after = (row_iota(K, K) > lane_iota(K, K)).astype(BF16)
    dots_ref[0:K] = before
    dots_ref[K : 2 * K] = after

    def owner_row(t):
        row = owner_ref[:, pl.ds(pl.multiple_of(t * K, K), K)]
        return jnp.where(lane_iota(1, K) < counts_ref[0, t], row, -1)

    def hot_place(t):
        row = owner_row(t)
        return hot16(2 * LANES, rank_ref[pl.ds(t, 1), :] + (row & 1) * LANES)

    def fetch(g, _):
        several = [unrolls[0] * g + i for i in range(unrolls[0])]
        hots = [hot_place(t) for t in several]
        spreads = [dot_nn(table_ref[...], jnp.concatenate([hot, hot], 0)) for hot in hots]
        for t, spread in zip(several, spreads):
            named = row_iota(half, K) == (owner_row(t) >> 1)
            for c in range(9):
                kept = jnp.where(named, spread[c * half : (c + 1) * half], 0.0)
                entry_ref[c, pl.ds(t, 1), :] = jnp.sum(kept, axis=0, keepdims=True)
        return 0

    lax.fori_loop(0, tiles // unrolls[0], fetch, 0)
    cx, cy = entry_ref[0] - 0.5, entry_ref[1] - 0.5
    a, b, c2 = entry_ref[2], entry_ref[3], entry_ref[4]
    opacity = 1.0 / (1.0 + jnp.exp(-entry_ref[8]))
    spots = lane_iota(1, K)
    left = jnp.concatenate([counts_ref[0, t] - spots for t in range(tiles)], 0)
    ax, ay = a * cx + b * cy, b * cx + c2 * cy
    base = jnp.log(0.99 * opacity) * LOG2E - (0.5 * LOG2E) * (ax * cx + ay * cy)
    coefs = [
        (-0.5 * LOG2E) * a,
        -LOG2E * b,
        (-0.5 * LOG2E) * c2,
        LOG2E * ax,
        LOG2E * ay,
        jnp.where(left > 0, base, -400.0),
    ]
    for i, coef in enumerate(coefs):
        coef_ref[:, i, :] = coef
    coef_ref[:, 6, :] = jnp.zeros_like(a)
    coef_ref[:, 7, :] = jnp.zeros_like(a)

    def scans(arrays, triangle):
        parts = [part for array in arrays for part in split2(array)]
        done = dot_nn(jnp.concatenate(parts, 0), triangle)
        pieces = [done[i * K : (i + 1) * K] for i in range(len(parts))]
        return [high + low for high, low in zip(pieces[0::2], pieces[1::2])]

    def shade(g, _):
        several = [unrolls[1] * g + i for i in range(unrolls[1])]
        blank, pad = jnp.zeros((8, K), BF16), jnp.zeros((4, K), F32)
        exponents = [
            dot_nn(pixel_columns, jnp.concatenate([*split3(coef_ref[t]), blank], 0))
            for t in several
        ]
        slopes, cot_rows = [], []
        for t in several:
            cot_high, cot_low = split2(cot_ref[t])
            ch, cl = cot_high.astype(F32), cot_low.astype(F32)
            cot_columns = jnp.concatenate([ch, ch, cl, cl, pad], 0).T.astype(BF16)
            colors = jnp.concatenate([entry_ref[c, pl.ds(t, 1), :] for c in range(5, 8)], 0)
            color_high, color_low = split2(colors)
            kh, kl = color_high.astype(F32), color_low.astype(F32)
            color_rows = jnp.concatenate([kh, kl, kh, kl, pad], 0).astype(BF16)
            slopes.append(dot_nn(cot_columns, color_rows))
            cot_rows.append(jnp.concatenate([ch, cl, pad[0:2]], 0).astype(BF16))
        alphas = [jnp.exp2(exponent) for exponent in exponents]
        log_keeps = [jnp.log(1.0 - alpha) for alpha in alphas]
        prefixes = scans(log_keeps, dots_ref[0:K])
        weights = [jnp.exp(prefix) * alpha for prefix, alpha in zip(prefixes, alphas)]
        pulls = [weight * slope for weight, slope in zip(weights, slopes)]
        suffixes = scans(pulls, dots_ref[K : 2 * K])
        for t, weight, rows in zip(several, weights, cot_rows):
            both = jnp.concatenate(split2(weight), 0)
            sums_ref[t, 8:16, :] = dot_nn(jnp.concatenate([rows, rows], 1), both)
        mass = jnp.concatenate([monomials, monomials], 1)
        for t, alpha, log_keep, pull, suffix in zip(several, alphas, log_keeps, pulls, suffixes):
            q = pull - alpha * jnp.exp(-log_keep) * suffix
            sums_ref[t, 0:8, :] = dot_nn(mass, jnp.concatenate(split2(q), 0))
        return 0

    lax.fori_loop(0, tiles // unrolls[1], shade, 0)
    mxx, mxy, myy, mx, my, m0 = [sums_ref[:, i, :] for i in range(6)]
    sx, sy = mx - cx * m0, my - cy * m0
    entry_ref[0] = a * sx + b * sy
    entry_ref[1] = b * sx + c2 * sy
    entry_ref[2] = -0.5 * (mxx - cx * (mx + sx))
    entry_ref[3] = -(mxy - cx * my - cy * sx)
    entry_ref[4] = -0.5 * (myy - cy * (my + sy))
    for i in range(3):
        entry_ref[5 + i] = sums_ref[:, 8 + i, :] + sums_ref[:, 11 + i, :]
    entry_ref[8] = (1.0 - opacity) * m0

    def give(g, _):
        sides, hots = [], []
        for i in range(unrolls[2]):
            t = unrolls[2] * g + i
            hot = hot_place(t)
            hits = hits16(half, owner_row(t) >> 1)
            placed = []
            for c in range(9):
                high, low = split2(entry_ref[c, pl.ds(t, 1), :])
                placed.append(jnp.concatenate([keep16(hits, high), keep16(hits, low)], 1))
            sides.append(jnp.concatenate(placed, 0))
            hots += [hot, hot]
        grad_ref[...] += dot_nt(jnp.concatenate(sides, 1), jnp.concatenate(hots, 1))
        return 0

    lax.fori_loop(0, tiles // unrolls[2], give, 0)
    for c in range(9):
        part = grad_ref[c * half : (c + 1) * half, :]
        out_ref[pl.ds(c, half, stride=18), :] = part[:, :LANES]
        out_ref[pl.ds(9 + c, half, stride=18), :] = part[:, LANES:]


def collect(ends_ref, vals_ref, first, number, held_ref):
    owners = vals_ref.shape[0] // 9
    base = owners * LANES - ends_ref[0, 2 * owners - 1]
    held_ref[...] = jnp.zeros_like(held_ref)
    blank = jnp.zeros((8 - number, LANES), F32)

    def row_at(g, j):
        rows = vals_ref[pl.ds(pl.multiple_of(g * 72, 8), 72), :]
        at = 9 * j + first
        return jnp.concatenate([rows[at : at + number], blank], 0)

    def store(bucket, at, block):
        held_ref[bucket, pl.ds(at, 1), :, :] = block[None]

    compact(owners, ends_ref, base, row_at, store)


def collect_kernel(ends_ref, vals_ref, look_ref, held_ref):
    collect(ends_ref, vals_ref, 5, 4, held_ref)
    look_ref[...] = held_ref[0, :, 0:4, :] + held_ref[1, :, 0:4, :]


def add_chunks(ids_ref, value_refs, totals, owners, acc_ref, transposed=False):
    def chunk(row, bucket, wide):
        sides, hots = [], []
        for at in range(0, wide, 2):
            first = row + at
            ids = ids_row(ids_ref, first)
            hot = hot_rows(ids, bucket)
            hits = hits16(LOW, ids & (LOW - 1))
            stacked = []
            for ref, number in value_refs[bucket]:
                for c in range(number):
                    pair = jnp.concatenate(
                        [ref[first, c : c + 1, :], ref[first + 1, c : c + 1, :]], 1
                    )
                    high, low = split2(pair)
                    stacked.append(
                        jnp.concatenate([keep16(hits, high), keep16(hits, low)], 1)
                    )
            sides.append(jnp.concatenate(stacked, 0))
            hots += [hot, hot]
        side, hot = jnp.concatenate(sides, 1), jnp.concatenate(hots, 1)
        if transposed:
            acc_ref[bucket] += dot_nt(hot, side)
        else:
            acc_ref[bucket] += dot_nt(side, hot)

    each_chunk(totals, owners, chunk)


def scatter_kernel(
    ends_ref, ids_ref, vals_ref, look_vals_ref, geo_ref, look_acc_ref, acc_ref, held_ref
):
    owners = vals_ref.shape[0] // 9
    totals = ends_ref[0, owners - 1], ends_ref[0, 2 * owners - 1]
    collect(ends_ref, vals_ref, 0, 5, held_ref)
    acc_ref[...] = jnp.zeros_like(acc_ref)
    values = [[(held_ref.at[bucket], 5), (look_vals_ref, 4)] for bucket in range(2)]
    add_chunks(ids_ref, values, totals, owners, acc_ref)
    for c in range(5):
        at = slice(c * LOW, (c + 1) * LOW)
        geo_ref[c] = jnp.concatenate([acc_ref[0, at], acc_ref[1, at]], 0).T
    for bucket in range(2):
        look_acc_ref[bucket] = acc_ref[bucket, 5 * LOW :, :].T


def add_view(ids_ref, vals_ref, start_ref, acc_ref):
    owners = vals_ref.shape[0] - 1
    place = ids_ref[owners + 1 : owners + 2, :]
    acc_ref[...] = start_ref[...]
    totals = place[0, owners - 1], place[0, 2 * owners - 1]
    add_chunks(ids_ref, [[(vals_ref, 4)]] * 2, totals, owners, acc_ref, transposed=True)


def finish_kernel(ids_ref, vals_ref, start_ref, look_ref, acc_ref):
    add_view(ids_ref, vals_ref, start_ref, acc_ref)
    for c in range(4):
        at = slice(c * LOW, (c + 1) * LOW)
        look_ref[:, c, :] = jnp.concatenate([acc_ref[0, :, at], acc_ref[1, :, at]], 1)


HBM = pl.BlockSpec(memory_space=pltpu.HBM)
VMEM = pl.BlockSpec(memory_space=pltpu.VMEM)
SMEM = pl.BlockSpec(memory_space=pltpu.SMEM)
LIMIT = pltpu.CompilerParams(vmem_limit_bytes=40 * 1024 * 1024)


def exchange(values, owners, axis="owner"):
    sent = values.reshape(owners, 1, -1)
    got = lax.all_to_all(sent, axis, split_axis=0, concat_axis=0, tiled=True)
    return got.reshape(values.shape)


def shards(geometry, appearance, list_owner, list_local, counts, cotangent):
    owners = lax.axis_size("owner")
    views = lax.axis_size("view")
    tiles = counts.shape[1]
    gauss = geometry.shape[2]
    rows = gauss // LANES
    target = list_owner.reshape(1, tiles * K)
    requests, ranks = pl.pallas_call(
        plan_kernel,
        out_shape=(
            jax.ShapeDtypeStruct((owners, LANES), jnp.int32),
            jax.ShapeDtypeStruct((tiles, K), jnp.int32),
        ),
        in_specs=[SMEM, HBM, HBM],
        out_specs=(VMEM, VMEM),
        scratch_shapes=[
            pltpu.VMEM((1, tiles * K), jnp.int32),
            pltpu.VMEM((1, tiles * K), jnp.int32),
            pltpu.SemaphoreType.DMA((2,)),
        ],
        compiler_params=pltpu.CompilerParams(vmem_limit_bytes=60 * 1024 * 1024),
    )(counts, target, list_local)
    table = pl.pallas_call(
        table_kernel,
        out_shape=jax.ShapeDtypeStruct((2, 9 * LOW, 512), BF16),
        in_specs=[VMEM, VMEM],
        out_specs=VMEM,
        compiler_params=LIMIT,
    )(geometry.reshape(5, rows, LANES), appearance.reshape(4, rows, LANES))
    asked = exchange(requests, owners)
    picked, packed = pl.pallas_call(
        gather_kernel,
        out_shape=(
            jax.ShapeDtypeStruct((owners * 9, LANES), F32),
            jax.ShapeDtypeStruct((owners + 8, LANES), jnp.int32),
        ),
        in_specs=[VMEM, VMEM],
        out_specs=(VMEM, VMEM),
        scratch_shapes=[
            pltpu.SMEM((8, LANES), jnp.int32),
            pltpu.VMEM((2, owners + 8, LANES), jnp.int32),
            pltpu.VMEM((2, owners + 2, 16, LANES), F32),
        ],
        compiler_params=LIMIT,
    )(asked, table)
    fetched = exchange(picked, owners)
    shifts = [[(i, (i + k) % views) for i in range(views)] for k in range(1, views)]
    other_ids = [lax.ppermute(packed, "view", shift) for shift in shifts]
    fetched, other_ids = lax.optimization_barrier((fetched, other_ids))
    outgoing = pl.pallas_call(
        functools.partial(tile_kernel, (16, 8, 16)),
        out_shape=jax.ShapeDtypeStruct((owners * 9, LANES), F32),
        in_specs=[SMEM, VMEM, VMEM, VMEM, VMEM],
        out_specs=VMEM,
        scratch_shapes=[
            pltpu.VMEM((9 * owners // 2, 4 * LANES), BF16),
            pltpu.VMEM((9 * owners // 2, 2 * LANES), F32),
            pltpu.VMEM((2 * K, K), BF16),
            pltpu.VMEM((9, tiles, K), F32),
            pltpu.VMEM((tiles, 8, K), F32),
            pltpu.VMEM((tiles, 16, K), F32),
        ],
        compiler_params=LIMIT,
    )(counts, target, ranks, cotangent[0], fetched)
    returned = exchange(outgoing, owners)
    ends = packed[owners + 1 :]
    look_vals = pl.pallas_call(
        collect_kernel,
        out_shape=jax.ShapeDtypeStruct((owners + 1, 4, LANES), F32),
        in_specs=[SMEM, VMEM],
        out_specs=VMEM,
        scratch_shapes=[pltpu.VMEM((2, owners + 1, 8, LANES), F32)],
        compiler_params=LIMIT,
    )(ends, returned)
    other_vals = [lax.ppermute(look_vals, "view", shift) for shift in shifts]
    sums = jax.ShapeDtypeStruct((2, 256, 4 * LOW), F32)
    geo, look = pl.pallas_call(
        scatter_kernel,
        out_shape=(jax.ShapeDtypeStruct((5, rows, LANES), F32), sums),
        in_specs=[SMEM, VMEM, VMEM, VMEM],
        out_specs=(VMEM, VMEM),
        scratch_shapes=[
            pltpu.VMEM((2, 9 * LOW, 256), F32),
            pltpu.VMEM((2, owners + 1, 8, LANES), F32),
        ],
        compiler_params=LIMIT,
    )(ends, packed, returned, look_vals)
    for i in reversed(range(views - 1)):
        last = i == 0
        look = pl.pallas_call(
            finish_kernel if last else add_view,
            out_shape=jax.ShapeDtypeStruct((rows, 4, LANES), F32) if last else sums,
            in_specs=[VMEM, VMEM, VMEM],
            out_specs=VMEM,
            scratch_shapes=[pltpu.VMEM((2, 256, 4 * LOW), F32)] if last else [],
            compiler_params=LIMIT,
        )(other_ids[i], other_vals[i], look)
    look = jnp.transpose(look, (1, 0, 2)).reshape(4, gauss)
    return (geo.reshape(1, 5, gauss), look)


def solution(mesh):
    placed = (
        P("view", None, "owner"),
        P(None, "owner"),
        P("view", "owner", None),
        P("view", "owner"),
        P("view", "owner"),
        P("view", "owner", None, None),
    )
    return jax.shard_map(
        shards,
        mesh=mesh,
        in_specs=placed,
        out_specs=(P("view", None, "owner"), P(None, "owner")),
        check_vma=False,
    )
```

```python
import functools
import math

import jax
import jax.numpy as jnp
from jax import lax
from jax.experimental import pallas as pl
from jax.experimental.pallas import tpu as pltpu
from jax.sharding import PartitionSpec as P

K = 256
TS = 16
LANES = 128
LOW = 64
F32 = jnp.float32
BF16 = jnp.bfloat16
LOG2E = 1.4426950408889634


def split2(x):
    high = x.astype(BF16)
    return high, (x - high.astype(F32)).astype(BF16)


def split3(x):
    high = x.astype(BF16)
    rest = x - high.astype(F32)
    middle = rest.astype(BF16)
    return high, middle, (rest - middle.astype(F32)).astype(BF16)


def dot_nn(a, b):
    return lax.dot_general(a, b, (((1,), (0,)), ((), ())), preferred_element_type=F32)


def dot_nt(a, b):
    return lax.dot_general(a, b, (((1,), (1,)), ((), ())), preferred_element_type=F32)


def row_iota(rows, columns):
    return lax.broadcasted_iota(jnp.int32, (rows, columns), 0)


def lane_iota(rows, columns):
    return lax.broadcasted_iota(jnp.int32, (rows, columns), 1)


def plan_kernel(
    counts_hbm,
    owner_hbm,
    local_hbm,
    request_ref,
    pair_ref,
    place_ref,
    counts_ref,
    owner_ref,
    local_ref,
    sem,
):
    copies = [
        pltpu.make_async_copy(counts_hbm, counts_ref, sem.at[0]),
        pltpu.make_async_copy(owner_hbm, owner_ref, sem.at[1]),
        pltpu.make_async_copy(local_hbm, local_ref, sem.at[2]),
    ]
    for copy in copies:
        copy.start()
    tiles = pair_ref.shape[0]
    owners = request_ref.shape[0]
    before = (row_iota(K, K) < lane_iota(K, K)).astype(BF16)
    for copy in copies:
        copy.wait()
    rows = [owner_ref[:, t * K : (t + 1) * K] for t in range(tiles)]
    rows = [
        jnp.where(lane_iota(1, K) < counts_ref[0, t], row, -1) for t, row in enumerate(rows)
    ]
    ids = [local_ref[:, t * K : (t + 1) * K] for t in range(tiles)]
    units = [jnp.where((i & LOW) != 0, 256.0, 1.0) for i in ids]
    found = [hits16(owners, row) for row in rows]
    halves = [keep16(f, jnp.ones((owners, K), BF16)) for f in found]
    scaled = [keep16(f, unit.astype(BF16)) for f, unit in zip(found, units)]
    inside = dot_nn(jnp.concatenate(scaled, 0), before)
    carry = jnp.zeros((owners, 1), F32)
    sides = []
    for t, row in enumerate(rows):
        named = row_iota(owners, K) == row
        here = inside[t * owners : (t + 1) * owners]
        both = jnp.sum(jnp.where(named, here + carry, 0.0), axis=0, keepdims=True)
        both = both.astype(jnp.int32)
        rank = jnp.where((ids[t] & LOW) != 0, LANES - 1 - (both >> 8), both & 255)
        carry = carry + jnp.sum(jnp.where(named, units[t], 0.0), axis=1, keepdims=True)
        pair_ref[t : t + 1, :] = row >> 1
        place_ref[t : t + 1, :] = rank + (row & 1) * LANES
        asked = ids[t] + 1
        hits = hits16(LANES, rank)
        high = keep16(hits, (asked >> 7).astype(F32).astype(BF16))
        low = keep16(hits, (asked & 127).astype(F32).astype(BF16))
        sides.append(jnp.concatenate([high, low], 0))
    total = dot_nt(jnp.concatenate(halves, 1), jnp.concatenate(sides, 1))
    request_ref[...] = (total[:, :LANES] * 128.0 + total[:, LANES:]).astype(jnp.int32)


def table_kernel(geo_ref, app_ref, table_ref):
    for c in range(9):
        values = geo_ref[c] if c < 5 else app_ref[c - 5]
        high, low = split2(values.T)
        for bucket in range(2):
            at = slice(bucket * LOW, (bucket + 1) * LOW)
            table_ref[bucket, c * LOW : (c + 1) * LOW, :] = jnp.concatenate(
                [high[at], low[at]], 1
            )


WIDE = 8


def ids_row(ref, at):
    return jnp.concatenate([ref[pl.ds(at, 1), :], ref[pl.ds(at + 1, 1), :]], 1) - 1


def hits16(rows, row):
    return lax.broadcasted_iota(jnp.int16, (rows, row.shape[1]), 0) == row.astype(jnp.int16)


def keep16(hits, row):
    return jnp.where(hits, row, jnp.zeros_like(row))


def hot16(rows, row):
    return keep16(hits16(rows, row), jnp.ones((rows, row.shape[1]), BF16))


def hot_rows(ids, bucket):
    fits = (ids >= 0) & (((ids >> 6) & 1) == bucket)
    return hot16(256, jnp.where(fits, ids >> 7, -1))


def low_mask(ids):
    return row_iota(LOW, 256) == (ids & (LOW - 1))


def each_chunk(totals, owners, chunk):
    most = jnp.maximum(totals[0], totals[1])
    steps = (most + 2 * LANES - 1) // (2 * LANES)
    large, left = (steps + 1) // 4, steps % 4

    def wide(j, _):
        chunk(WIDE * j, 0, WIDE)
        chunk(owners - WIDE * (j + 1), 1, WIDE)
        return 0

    lax.fori_loop(0, large, wide, 0)
    for units in (1, 2):

        @pl.when(left == units)
        def _():
            chunk(WIDE * large, 0, 2 * units)
            chunk(owners - WIDE * large - 2 * units, 1, 2 * units)


def compact(owners, ends_ref, base, row_at, store):
    blank = jnp.zeros((8, LANES), row_at(0, 0).dtype)
    lanes = lane_iota(8, LANES)

    def group(g, carry):
        carry = list(carry)
        for j in range(8):
            s = g * 8 + j
            row = row_at(g, j)
            for bucket in range(2):
                offset, now = carry[bucket]
                end = ends_ref[0, bucket * owners + s] + (base if bucket else 0)
                if bucket == 0:
                    part = jnp.where(lanes < end - offset, row, blank)
                    rolled = pltpu.roll(part, offset & 127, 1)
                else:
                    part = jnp.where(lanes >= LANES - (end - offset), row, blank)
                    rolled = pltpu.roll(part, end & 127, 1)
                fits = lanes >= (offset & 127)
                block = now + jnp.where(fits, rolled, blank)
                spilt = jnp.where(fits, blank, rolled)
                store(bucket, offset >> 7, block)
                carry[bucket] = end, jnp.where((end >> 7) > (offset >> 7), spilt, block)
        return tuple(carry)

    carry = lax.fori_loop(0, owners // 8, group, ((0, blank), (base, blank)))
    for bucket, (offset, now) in enumerate(carry):
        store(bucket, offset >> 7, now)


def gather_kernel(asked_ref, table_ref, out_ref, packed_ref, ends_ref, held_ref, found_ref):
    owners = asked_ref.shape[0]
    asked = asked_ref[...]
    odd = ((asked - 1) & LOW) != 0
    valid = [(asked > 0) & ~odd, (asked > 0) & odd]
    valid = jnp.concatenate([v.astype(F32).astype(BF16) for v in valid], 1)
    upto = (row_iota(owners, owners) >= lane_iota(owners, owners)).astype(F32).astype(BF16)
    sides = ((lane_iota(8, 2 * LANES) >> 7) == row_iota(8, 2 * LANES)).astype(F32).astype(BF16)
    ends = dot_nt(sides, dot_nn(upto, valid).astype(BF16)).astype(jnp.int32)
    held_ref[...] = jnp.zeros_like(held_ref)
    for s in range(owners):
        ends_ref[0, s] = ends[0, s]
        ends_ref[0, owners + s] = ends[1, s]
    totals = ends[0, owners - 1], ends[1, owners - 1]
    base = owners * LANES - totals[1]

    def row_at(g, j):
        return jnp.broadcast_to(asked_ref[pl.ds(g * 8 + j, 1), :], (8, LANES))

    def store(bucket, at, block):
        held_ref[bucket, pl.ds(at, 1), :] = block[0:1]

    compact(owners, ends_ref, base, row_at, store)
    packed_ref[...] = held_ref[0] + held_ref[1]
    packed_ref[owners + 1 : owners + 2, 0 : 2 * owners] = jnp.concatenate(
        [ends[0:1], ends[1:2]], 1
    )

    def chunk(row, bucket, wide):
        for at in range(0, wide, 2):
            ids = ids_row(held_ref.at[bucket], row + at)
            hot = hot_rows(ids, bucket)
            found = dot_nn(table_ref[bucket], jnp.concatenate([hot, hot], 0))
            mask = low_mask(ids)
            rows = [
                jnp.sum(jnp.where(mask, found[c * LOW : (c + 1) * LOW], 0.0), axis=0, keepdims=True)
                for c in range(9)
            ]
            values = jnp.concatenate(rows, 0)
            found_ref[bucket, row + at + 1, 0:9, :] = values[:, :LANES]
            found_ref[bucket, row + at + 2, 0:9, :] = values[:, LANES:]

    each_chunk(totals, owners, chunk)

    def expand(g, offsets):
        lanes = lane_iota(16, LANES)
        low, high = offsets
        blocks = []
        for j in range(8):
            s = g * 8 + j
            low_end, high_end = ends_ref[0, s], base + ends_ref[0, owners + s]
            sources = []
            for bucket, at, row in ((0, low, (low >> 7) + 1), (1, high_end, high_end >> 7)):
                back = (LANES - (at & 127)) & 127
                first = pltpu.roll(found_ref[bucket, row], back, 1)
                second = pltpu.roll(found_ref[bucket, row + 1], back, 1)
                sources.append(jnp.where(lanes + (at & 127) < LANES, first, second))
            values = jnp.where(lanes >= LANES - (high_end - high), sources[1], 0.0)
            values = jnp.where(lanes < low_end - low, sources[0], values)
            blocks.append(values[0:9])
            low, high = low_end, high_end
        out_ref[pl.ds(pl.multiple_of(g * 72, 8), 72), :] = jnp.concatenate(blocks, 0)
        return low, high

    lax.fori_loop(0, owners // 8, expand, (0, base))


def pixel_rows():
    pixel = lane_iota(1, K)
    u = ((pixel & (TS - 1)).astype(F32) + 0.5) / TS - 0.5
    v = ((pixel >> 4).astype(F32) + 0.5) / TS - 0.5
    one = jnp.ones((1, K), F32)
    zero = jnp.zeros((2, K), F32)
    return jnp.concatenate([u * u, u * v, v * v, u, v, one, zero], 0)


def tile_kernel(
    unrolls,
    pair_ref,
    place_ref,
    cot_ref,
    fetched_ref,
    out_ref,
    table_ref,
    grad_ref,
    dots_ref,
    entry_ref,
    coef_ref,
    sums_ref,
):
    tiles = pair_ref.shape[0]
    owners = fetched_ref.shape[0] // 9
    unrolls = [math.gcd(tiles, n) for n in unrolls]
    half = owners // 2
    for c in range(9):
        even = fetched_ref[pl.ds(c, half, stride=18), :]
        odd = fetched_ref[pl.ds(9 + c, half, stride=18), :]
        high, low = split2(jnp.concatenate([even, odd], 1))
        table_ref[c * half : (c + 1) * half, :] = jnp.concatenate([high, low], 1)
    grad_ref[...] = jnp.zeros_like(grad_ref)
    pixels = pixel_rows()
    monomials = pixels.astype(BF16)
    pixel_columns = jnp.concatenate([pixels] * 4, 0).T.astype(BF16)
    before = (row_iota(K, K) < lane_iota(K, K)).astype(BF16)
    after = (row_iota(K, K) > lane_iota(K, K)).astype(BF16)
    dots_ref[0:K] = before
    dots_ref[K : 2 * K] = after

    def hot_place(t):
        return hot16(2 * LANES, place_ref[pl.ds(t, 1), :])

    def fetch(g, _):
        several = [unrolls[0] * g + i for i in range(unrolls[0])]
        hots = [hot_place(t) for t in several]
        spreads = [dot_nn(table_ref[...], jnp.concatenate([hot, hot], 0)) for hot in hots]
        for t, spread in zip(several, spreads):
            named = row_iota(half, K) == pair_ref[pl.ds(t, 1), :]
            for c in range(9):
                kept = jnp.where(named, spread[c * half : (c + 1) * half], 0.0)
                entry_ref[c, pl.ds(t, 1), :] = jnp.sum(kept, axis=0, keepdims=True)
        return 0

    lax.fori_loop(0, tiles // unrolls[0], fetch, 0)
    cx, cy = entry_ref[0] - 0.5, entry_ref[1] - 0.5
    a, b, c2 = entry_ref[2], entry_ref[3], entry_ref[4]
    opacity = 1.0 / (1.0 + jnp.exp(-entry_ref[8]))
    ax, ay = a * cx + b * cy, b * cx + c2 * cy
    base = jnp.log(0.99 * opacity) * LOG2E - (0.5 * LOG2E) * (ax * cx + ay * cy)
    coefs = [
        (-0.5 * LOG2E) * a,
        -LOG2E * b,
        (-0.5 * LOG2E) * c2,
        LOG2E * ax,
        LOG2E * ay,
        jnp.where(pair_ref[...] >= 0, base, -400.0),
    ]
    for i, coef in enumerate(coefs):
        coef_ref[:, i, :] = coef
    coef_ref[:, 6, :] = jnp.zeros_like(a)
    coef_ref[:, 7, :] = jnp.zeros_like(a)

    def scans(arrays, triangle):
        parts = [part for array in arrays for part in split2(array)]
        done = dot_nn(jnp.concatenate(parts, 0), triangle)
        pieces = [done[i * K : (i + 1) * K] for i in range(len(parts))]
        return [high + low for high, low in zip(pieces[0::2], pieces[1::2])]

    def shade(g, _):
        several = [unrolls[1] * g + i for i in range(unrolls[1])]
        blank, pad = jnp.zeros((8, K), BF16), jnp.zeros((4, K), F32)
        exponents = [
            dot_nn(pixel_columns, jnp.concatenate([*split3(coef_ref[t]), blank], 0))
            for t in several
        ]
        slopes, cot_rows = [], []
        for t in several:
            cot_high, cot_low = split2(cot_ref[t])
            ch, cl = cot_high.astype(F32), cot_low.astype(F32)
            cot_columns = jnp.concatenate([ch, ch, cl, cl, pad], 0).T.astype(BF16)
            colors = jnp.concatenate([entry_ref[c, pl.ds(t, 1), :] for c in range(5, 8)], 0)
            color_high, color_low = split2(colors)
            kh, kl = color_high.astype(F32), color_low.astype(F32)
            color_rows = jnp.concatenate([kh, kl, kh, kl, pad], 0).astype(BF16)
            slopes.append(dot_nn(cot_columns, color_rows))
            cot_rows.append(jnp.concatenate([ch, cl, pad[0:2]], 0).astype(BF16))
        alphas = [jnp.exp2(exponent) for exponent in exponents]
        log_keeps = [jnp.log(1.0 - alpha) for alpha in alphas]
        prefixes = scans(log_keeps, dots_ref[0:K])
        weights = [jnp.exp(prefix) * alpha for prefix, alpha in zip(prefixes, alphas)]
        pulls = [weight * slope for weight, slope in zip(weights, slopes)]
        suffixes = scans(pulls, dots_ref[K : 2 * K])
        for t, weight, rows in zip(several, weights, cot_rows):
            both = jnp.concatenate(split2(weight), 0)
            sums_ref[t, 8:16, :] = dot_nn(jnp.concatenate([rows, rows], 1), both)
        mass = jnp.concatenate([monomials, monomials], 1)
        for t, alpha, log_keep, pull, suffix in zip(several, alphas, log_keeps, pulls, suffixes):
            q = pull - alpha * jnp.exp(-log_keep) * suffix
            sums_ref[t, 0:8, :] = dot_nn(mass, jnp.concatenate(split2(q), 0))
        return 0

    lax.fori_loop(0, tiles // unrolls[1], shade, 0)
    mxx, mxy, myy, mx, my, m0 = [sums_ref[:, i, :] for i in range(6)]
    sx, sy = mx - cx * m0, my - cy * m0
    entry_ref[0] = a * sx + b * sy
    entry_ref[1] = b * sx + c2 * sy
    entry_ref[2] = -0.5 * (mxx - cx * (mx + sx))
    entry_ref[3] = -(mxy - cx * my - cy * sx)
    entry_ref[4] = -0.5 * (myy - cy * (my + sy))
    for i in range(3):
        entry_ref[5 + i] = sums_ref[:, 8 + i, :] + sums_ref[:, 11 + i, :]
    entry_ref[8] = (1.0 - opacity) * m0

    def give(g, _):
        sides, hots = [], []
        for i in range(unrolls[2]):
            t = unrolls[2] * g + i
            hot = hot_place(t)
            hits = hits16(half, pair_ref[pl.ds(t, 1), :])
            placed = []
            for c in range(9):
                high, low = split2(entry_ref[c, pl.ds(t, 1), :])
                placed.append(jnp.concatenate([keep16(hits, high), keep16(hits, low)], 1))
            sides.append(jnp.concatenate(placed, 0))
            hots += [hot, hot]
        grad_ref[...] += dot_nt(jnp.concatenate(sides, 1), jnp.concatenate(hots, 1))
        return 0

    lax.fori_loop(0, tiles // unrolls[2], give, 0)
    for c in range(9):
        part = grad_ref[c * half : (c + 1) * half, :]
        out_ref[pl.ds(c, half, stride=18), :] = part[:, :LANES]
        out_ref[pl.ds(9 + c, half, stride=18), :] = part[:, LANES:]


def collect(ends_ref, vals_ref, first, number, held_ref):
    owners = vals_ref.shape[0] // 9
    base = owners * LANES - ends_ref[0, 2 * owners - 1]
    held_ref[...] = jnp.zeros_like(held_ref)
    blank = jnp.zeros((8 - number, LANES), F32)

    def row_at(g, j):
        rows = vals_ref[pl.ds(pl.multiple_of(g * 72, 8), 72), :]
        at = 9 * j + first
        return jnp.concatenate([rows[at : at + number], blank], 0)

    def store(bucket, at, block):
        held_ref[bucket, pl.ds(at, 1), :, :] = block[None]

    compact(owners, ends_ref, base, row_at, store)


def collect_kernel(ends_ref, vals_ref, look_ref, held_ref):
    collect(ends_ref, vals_ref, 5, 4, held_ref)
    look_ref[...] = held_ref[0, :, 0:4, :] + held_ref[1, :, 0:4, :]


def add_chunks(ids_ref, value_refs, totals, owners, acc_ref, transposed=False):
    def chunk(row, bucket, wide):
        sides, hots = [], []
        for at in range(0, wide, 2):
            first = row + at
            ids = ids_row(ids_ref, first)
            hot = hot_rows(ids, bucket)
            hits = hits16(LOW, ids & (LOW - 1))
            stacked = []
            for ref, number in value_refs[bucket]:
                for c in range(number):
                    pair = jnp.concatenate(
                        [ref[first, c : c + 1, :], ref[first + 1, c : c + 1, :]], 1
                    )
                    high, low = split2(pair)
                    stacked.append(
                        jnp.concatenate([keep16(hits, high), keep16(hits, low)], 1)
                    )
            sides.append(jnp.concatenate(stacked, 0))
            hots += [hot, hot]
        side, hot = jnp.concatenate(sides, 1), jnp.concatenate(hots, 1)
        if transposed:
            acc_ref[bucket] += dot_nt(hot, side)
        else:
            acc_ref[bucket] += dot_nt(side, hot)

    each_chunk(totals, owners, chunk)


def scatter_kernel(
    ends_ref, ids_ref, vals_ref, look_vals_ref, geo_ref, look_acc_ref, acc_ref, held_ref
):
    owners = vals_ref.shape[0] // 9
    totals = ends_ref[0, owners - 1], ends_ref[0, 2 * owners - 1]
    collect(ends_ref, vals_ref, 0, 5, held_ref)
    acc_ref[...] = jnp.zeros_like(acc_ref)
    values = [[(held_ref.at[bucket], 5), (look_vals_ref, 4)] for bucket in range(2)]
    add_chunks(ids_ref, values, totals, owners, acc_ref)
    for c in range(5):
        at = slice(c * LOW, (c + 1) * LOW)
        geo_ref[c] = jnp.concatenate([acc_ref[0, at], acc_ref[1, at]], 0).T
    for bucket in range(2):
        look_acc_ref[bucket] = acc_ref[bucket, 5 * LOW :, :].T


def add_view(ids_ref, vals_ref, start_ref, acc_ref):
    owners = vals_ref.shape[0] - 1
    place = ids_ref[owners + 1 : owners + 2, :]
    acc_ref[...] = start_ref[...]
    totals = place[0, owners - 1], place[0, 2 * owners - 1]
    add_chunks(ids_ref, [[(vals_ref, 4)]] * 2, totals, owners, acc_ref, transposed=True)


def finish_kernel(ids_ref, vals_ref, start_ref, look_ref, acc_ref):
    add_view(ids_ref, vals_ref, start_ref, acc_ref)
    for c in range(4):
        at = slice(c * LOW, (c + 1) * LOW)
        look_ref[:, c, :] = jnp.concatenate([acc_ref[0, :, at], acc_ref[1, :, at]], 1)


HBM = pl.BlockSpec(memory_space=pltpu.HBM)
VMEM = pl.BlockSpec(memory_space=pltpu.VMEM)
SMEM = pl.BlockSpec(memory_space=pltpu.SMEM)
LIMIT = pltpu.CompilerParams(vmem_limit_bytes=40 * 1024 * 1024)


def exchange(values, owners, axis="owner"):
    sent = values.reshape(owners, 1, -1)
    got = lax.all_to_all(sent, axis, split_axis=0, concat_axis=0, tiled=True)
    return got.reshape(values.shape)


def shards(geometry, appearance, list_owner, list_local, counts, cotangent):
    owners = lax.axis_size("owner")
    views = lax.axis_size("view")
    tiles = counts.shape[1]
    gauss = geometry.shape[2]
    rows = gauss // LANES
    target = list_owner.reshape(1, tiles * K)
    requests, pairs, places = pl.pallas_call(
        plan_kernel,
        out_shape=(
            jax.ShapeDtypeStruct((owners, LANES), jnp.int32),
            jax.ShapeDtypeStruct((tiles, K), jnp.int32),
            jax.ShapeDtypeStruct((tiles, K), jnp.int32),
        ),
        in_specs=[HBM, HBM, HBM],
        out_specs=(VMEM, VMEM, VMEM),
        scratch_shapes=[
            pltpu.SMEM((1, tiles), jnp.int32),
            pltpu.VMEM((1, tiles * K), jnp.int32),
            pltpu.VMEM((1, tiles * K), jnp.int32),
            pltpu.SemaphoreType.DMA((3,)),
        ],
        compiler_params=pltpu.CompilerParams(vmem_limit_bytes=60 * 1024 * 1024),
    )(counts, target, list_local)
    table = pl.pallas_call(
        table_kernel,
        out_shape=jax.ShapeDtypeStruct((2, 9 * LOW, 512), BF16),
        in_specs=[VMEM, VMEM],
        out_specs=VMEM,
        compiler_params=LIMIT,
    )(geometry.reshape(5, rows, LANES), appearance.reshape(4, rows, LANES))
    asked = exchange(requests, owners)
    picked, packed = pl.pallas_call(
        gather_kernel,
        out_shape=(
            jax.ShapeDtypeStruct((owners * 9, LANES), F32),
            jax.ShapeDtypeStruct((owners + 8, LANES), jnp.int32),
        ),
        in_specs=[VMEM, VMEM],
        out_specs=(VMEM, VMEM),
        scratch_shapes=[
            pltpu.SMEM((8, LANES), jnp.int32),
            pltpu.VMEM((2, owners + 8, LANES), jnp.int32),
            pltpu.VMEM((2, owners + 2, 16, LANES), F32),
        ],
        compiler_params=LIMIT,
    )(asked, table)
    fetched = exchange(picked, owners)
    shifts = [[(i, (i + k) % views) for i in range(views)] for k in range(1, views)]
    other_ids = [lax.ppermute(packed, "view", shift) for shift in shifts]
    fetched, other_ids = lax.optimization_barrier((fetched, other_ids))
    outgoing = pl.pallas_call(
        functools.partial(tile_kernel, (16, 8, 16)),
        out_shape=jax.ShapeDtypeStruct((owners * 9, LANES), F32),
        in_specs=[VMEM, VMEM, VMEM, VMEM],
        out_specs=VMEM,
        scratch_shapes=[
            pltpu.VMEM((9 * owners // 2, 4 * LANES), BF16),
            pltpu.VMEM((9 * owners // 2, 2 * LANES), F32),
            pltpu.VMEM((2 * K, K), BF16),
            pltpu.VMEM((9, tiles, K), F32),
            pltpu.VMEM((tiles, 8, K), F32),
            pltpu.VMEM((tiles, 16, K), F32),
        ],
        compiler_params=LIMIT,
    )(pairs, places, cotangent[0], fetched)
    returned = exchange(outgoing, owners)
    ends = packed[owners + 1 :]
    look_vals = pl.pallas_call(
        collect_kernel,
        out_shape=jax.ShapeDtypeStruct((owners + 1, 4, LANES), F32),
        in_specs=[SMEM, VMEM],
        out_specs=VMEM,
        scratch_shapes=[pltpu.VMEM((2, owners + 1, 8, LANES), F32)],
        compiler_params=LIMIT,
    )(ends, returned)
    other_vals = [lax.ppermute(look_vals, "view", shift) for shift in shifts]
    sums = jax.ShapeDtypeStruct((2, 256, 4 * LOW), F32)
    geo, look = pl.pallas_call(
        scatter_kernel,
        out_shape=(jax.ShapeDtypeStruct((5, rows, LANES), F32), sums),
        in_specs=[SMEM, VMEM, VMEM, VMEM],
        out_specs=(VMEM, VMEM),
        scratch_shapes=[
            pltpu.VMEM((2, 9 * LOW, 256), F32),
            pltpu.VMEM((2, owners + 1, 8, LANES), F32),
        ],
        compiler_params=LIMIT,
    )(ends, packed, returned, look_vals)
    for i in reversed(range(views - 1)):
        last = i == 0
        look = pl.pallas_call(
            finish_kernel if last else add_view,
            out_shape=jax.ShapeDtypeStruct((rows, 4, LANES), F32) if last else sums,
            in_specs=[VMEM, VMEM, VMEM],
            out_specs=VMEM,
            scratch_shapes=[pltpu.VMEM((2, 256, 4 * LOW), F32)] if last else [],
            compiler_params=LIMIT,
        )(other_ids[i], other_vals[i], look)
    look = jnp.transpose(look, (1, 0, 2)).reshape(4, gauss)
    return (geo.reshape(1, 5, gauss), look)


def solution(mesh):
    placed = (
        P("view", None, "owner"),
        P(None, "owner"),
        P("view", "owner", None),
        P("view", "owner"),
        P("view", "owner"),
        P("view", "owner", None, None),
    )
    return jax.shard_map(
        shards,
        mesh=mesh,
        in_specs=placed,
        out_specs=(P("view", None, "owner"), P(None, "owner")),
        check_vma=False,
    )
```

```python
import functools
import math

import jax
import jax.numpy as jnp
from jax import lax
from jax.experimental import pallas as pl
from jax.experimental.pallas import tpu as pltpu
from jax.sharding import PartitionSpec as P

K = 256
TS = 16
LANES = 128
LOW = 64
F32 = jnp.float32
BF16 = jnp.bfloat16
LOG2E = 1.4426950408889634


def split2(x):
    high = x.astype(BF16)
    return high, (x - high.astype(F32)).astype(BF16)


def split3(x):
    high = x.astype(BF16)
    rest = x - high.astype(F32)
    middle = rest.astype(BF16)
    return high, middle, (rest - middle.astype(F32)).astype(BF16)


def dot_nn(a, b):
    return lax.dot_general(a, b, (((1,), (0,)), ((), ())), preferred_element_type=F32)


def dot_nt(a, b):
    return lax.dot_general(a, b, (((1,), (1,)), ((), ())), preferred_element_type=F32)


def row_iota(rows, columns):
    return lax.broadcasted_iota(jnp.int32, (rows, columns), 0)


def lane_iota(rows, columns):
    return lax.broadcasted_iota(jnp.int32, (rows, columns), 1)


def plan_kernel(
    counts_hbm,
    owner_hbm,
    local_hbm,
    request_ref,
    pair_ref,
    place_ref,
    counts_ref,
    owner_ref,
    local_ref,
    sem,
):
    copies = [
        pltpu.make_async_copy(counts_hbm, counts_ref, sem.at[0]),
        pltpu.make_async_copy(owner_hbm, owner_ref, sem.at[1]),
        pltpu.make_async_copy(local_hbm, local_ref, sem.at[2]),
    ]
    for copy in copies:
        copy.start()
    tiles = pair_ref.shape[0]
    owners = request_ref.shape[0]
    before = (row_iota(K, K) < lane_iota(K, K)).astype(BF16)
    for copy in copies:
        copy.wait()
    rows = [owner_ref[:, t * K : (t + 1) * K] for t in range(tiles)]
    rows = [
        jnp.where(lane_iota(1, K) < counts_ref[0, t], row, -1) for t, row in enumerate(rows)
    ]
    ids = [local_ref[:, t * K : (t + 1) * K] for t in range(tiles)]
    units = [jnp.where((i & LOW) != 0, 256.0, 1.0) for i in ids]
    found = [hits16(owners, row) for row in rows]
    halves = [keep16(f, jnp.ones((owners, K), BF16)) for f in found]
    scaled = [keep16(f, unit.astype(BF16)) for f, unit in zip(found, units)]
    inside = dot_nn(jnp.concatenate(scaled, 0), before)
    carry = jnp.zeros((owners, 1), F32)
    sides = []
    for t, row in enumerate(rows):
        named = row_iota(owners, K) == row
        here = inside[t * owners : (t + 1) * owners]
        both = jnp.sum(jnp.where(named, here + carry, 0.0), axis=0, keepdims=True)
        both = both.astype(jnp.int32)
        rank = jnp.where((ids[t] & LOW) != 0, LANES - 1 - (both >> 8), both & 255)
        carry = carry + jnp.sum(jnp.where(named, units[t], 0.0), axis=1, keepdims=True)
        pair_ref[t : t + 1, :] = row >> 1
        place_ref[t : t + 1, :] = rank + (row & 1) * LANES
        asked = ids[t] + 1
        hits = hits16(LANES, rank)
        high = keep16(hits, (asked >> 7).astype(F32).astype(BF16))
        low = keep16(hits, (asked & 127).astype(F32).astype(BF16))
        sides.append(jnp.concatenate([high, low], 0))
    total = dot_nt(jnp.concatenate(halves, 1), jnp.concatenate(sides, 1))
    request_ref[...] = (total[:, :LANES] * 128.0 + total[:, LANES:]).astype(jnp.int32)


def table_kernel(geo_ref, app_ref, table_ref):
    for c in range(9):
        values = geo_ref[c] if c < 5 else app_ref[c - 5]
        high, low = split2(values.T)
        for bucket in range(2):
            at = slice(bucket * LOW, (bucket + 1) * LOW)
            table_ref[bucket, c * LOW : (c + 1) * LOW, :] = jnp.concatenate(
                [high[at], low[at]], 1
            )


WIDE = 8


def ids_row(ref, at):
    return jnp.concatenate([ref[pl.ds(at, 1), :], ref[pl.ds(at + 1, 1), :]], 1) - 1


def hits16(rows, row):
    return lax.broadcasted_iota(jnp.int16, (rows, row.shape[1]), 0) == row.astype(jnp.int16)


def keep16(hits, row):
    return jnp.where(hits, row, jnp.zeros_like(row))


def hot16(rows, row):
    return keep16(hits16(rows, row), jnp.ones((rows, row.shape[1]), BF16))


def hot_rows(ids, bucket):
    fits = (ids >= 0) & (((ids >> 6) & 1) == bucket)
    return hot16(256, jnp.where(fits, ids >> 7, -1))


def low_mask(ids):
    return row_iota(LOW, 256) == (ids & (LOW - 1))


def each_chunk(totals, owners, chunk):
    most = jnp.maximum(totals[0], totals[1])
    steps = (most + 2 * LANES - 1) // (2 * LANES)
    large, left = (steps + 1) // 4, steps % 4

    def wide(j, _):
        chunk(WIDE * j, 0, WIDE)
        chunk(owners - WIDE * (j + 1), 1, WIDE)
        return 0

    lax.fori_loop(0, large, wide, 0)
    for units in (1, 2):

        @pl.when(left == units)
        def _():
            chunk(WIDE * large, 0, 2 * units)
            chunk(owners - WIDE * large - 2 * units, 1, 2 * units)


def compact(owners, ends_ref, base, row_at, store):
    blank = jnp.zeros((8, LANES), row_at(0, 0).dtype)
    lanes = lane_iota(8, LANES)

    def group(g, carry):
        carry = list(carry)
        for j in range(8):
            s = g * 8 + j
            row = row_at(g, j)
            for bucket in range(2):
                offset, now = carry[bucket]
                end = ends_ref[0, bucket * owners + s] + (base if bucket else 0)
                if bucket == 0:
                    part = jnp.where(lanes < end - offset, row, blank)
                    rolled = pltpu.roll(part, offset & 127, 1)
                else:
                    part = jnp.where(lanes >= LANES - (end - offset), row, blank)
                    rolled = pltpu.roll(part, end & 127, 1)
                fits = lanes >= (offset & 127)
                block = now + jnp.where(fits, rolled, blank)
                spilt = jnp.where(fits, blank, rolled)
                store(bucket, offset >> 7, block)
                carry[bucket] = end, jnp.where((end >> 7) > (offset >> 7), spilt, block)
        return tuple(carry)

    carry = lax.fori_loop(0, owners // 8, group, ((0, blank), (base, blank)))
    for bucket, (offset, now) in enumerate(carry):
        store(bucket, offset >> 7, now)


def to_scalars(ends, ends_ref):
    amount = ends.shape[1]
    for s in range(amount):
        ends_ref[0, s] = ends[0, s]
    return ends[0, amount // 2 - 1], ends[0, amount - 1]


def gather_kernel(asked_ref, table_ref, out_ref, packed_ref, ends_ref, held_ref, found_ref):
    owners = asked_ref.shape[0]
    asked = asked_ref[...]
    odd = ((asked - 1) & LOW) != 0
    valid = [(asked > 0) & ~odd, (asked > 0) & odd]
    valid = jnp.concatenate([v.astype(F32).astype(BF16) for v in valid], 1)
    upto = (row_iota(owners, owners) >= lane_iota(owners, owners)).astype(F32).astype(BF16)
    sides = ((lane_iota(8, 2 * LANES) >> 7) == row_iota(8, 2 * LANES)).astype(F32).astype(BF16)
    ends = dot_nt(sides, dot_nn(upto, valid).astype(BF16)).astype(jnp.int32)
    held_ref[...] = jnp.zeros_like(held_ref)
    ends = jnp.concatenate([ends[0:1], ends[1:2]], 1)
    totals = to_scalars(ends, ends_ref)
    base = owners * LANES - totals[1]

    def row_at(g, j):
        return jnp.broadcast_to(asked_ref[pl.ds(g * 8 + j, 1), :], (8, LANES))

    def store(bucket, at, block):
        held_ref[bucket, pl.ds(at, 1), :] = block[0:1]

    compact(owners, ends_ref, base, row_at, store)
    packed_ref[...] = held_ref[0] + held_ref[1]
    packed_ref[owners + 1 : owners + 2, 0 : 2 * owners] = ends

    def chunk(row, bucket, wide):
        for at in range(0, wide, 2):
            ids = ids_row(held_ref.at[bucket], row + at)
            hot = hot_rows(ids, bucket)
            found = dot_nn(table_ref[bucket], jnp.concatenate([hot, hot], 0))
            mask = low_mask(ids)
            rows = [
                jnp.sum(jnp.where(mask, found[c * LOW : (c + 1) * LOW], 0.0), axis=0, keepdims=True)
                for c in range(9)
            ]
            values = jnp.concatenate(rows, 0)
            found_ref[bucket, row + at + 1, 0:9, :] = values[:, :LANES]
            found_ref[bucket, row + at + 2, 0:9, :] = values[:, LANES:]

    each_chunk(totals, owners, chunk)

    def expand(g, offsets):
        lanes = lane_iota(16, LANES)
        low, high = offsets
        blocks = []
        for j in range(8):
            s = g * 8 + j
            low_end, high_end = ends_ref[0, s], base + ends_ref[0, owners + s]
            sources = []
            for bucket, at, row in ((0, low, (low >> 7) + 1), (1, high_end, high_end >> 7)):
                back = (LANES - (at & 127)) & 127
                first = pltpu.roll(found_ref[bucket, row], back, 1)
                second = pltpu.roll(found_ref[bucket, row + 1], back, 1)
                sources.append(jnp.where(lanes + (at & 127) < LANES, first, second))
            values = jnp.where(lanes >= LANES - (high_end - high), sources[1], 0.0)
            values = jnp.where(lanes < low_end - low, sources[0], values)
            blocks.append(values[0:9])
            low, high = low_end, high_end
        out_ref[pl.ds(pl.multiple_of(g * 72, 8), 72), :] = jnp.concatenate(blocks, 0)
        return low, high

    lax.fori_loop(0, owners // 8, expand, (0, base))


def pixel_rows():
    pixel = lane_iota(1, K)
    u = ((pixel & (TS - 1)).astype(F32) + 0.5) / TS - 0.5
    v = ((pixel >> 4).astype(F32) + 0.5) / TS - 0.5
    one = jnp.ones((1, K), F32)
    zero = jnp.zeros((2, K), F32)
    return jnp.concatenate([u * u, u * v, v * v, u, v, one, zero], 0)


def tile_kernel(
    unrolls,
    pair_ref,
    place_ref,
    cot_ref,
    fetched_ref,
    out_ref,
    table_ref,
    grad_ref,
    dots_ref,
    entry_ref,
    coef_ref,
    sums_ref,
):
    tiles = pair_ref.shape[0]
    owners = fetched_ref.shape[0] // 9
    unrolls = [math.gcd(tiles, n) for n in unrolls]
    half = owners // 2
    for c in range(9):
        even = fetched_ref[pl.ds(c, half, stride=18), :]
        odd = fetched_ref[pl.ds(9 + c, half, stride=18), :]
        high, low = split2(jnp.concatenate([even, odd], 1))
        table_ref[c * half : (c + 1) * half, :] = jnp.concatenate([high, low], 1)
    grad_ref[...] = jnp.zeros_like(grad_ref)
    pixels = pixel_rows()
    monomials = pixels.astype(BF16)
    pixel_columns = jnp.concatenate([pixels] * 4, 0).T.astype(BF16)
    before = (row_iota(K, K) < lane_iota(K, K)).astype(BF16)
    after = (row_iota(K, K) > lane_iota(K, K)).astype(BF16)
    dots_ref[0:K] = before
    dots_ref[K : 2 * K] = after

    def hot_place(t):
        return hot16(2 * LANES, place_ref[pl.ds(t, 1), :])

    def fetch(g, _):
        several = [unrolls[0] * g + i for i in range(unrolls[0])]
        hots = [hot_place(t) for t in several]
        spreads = [dot_nn(table_ref[...], jnp.concatenate([hot, hot], 0)) for hot in hots]
        for t, spread in zip(several, spreads):
            named = row_iota(half, K) == pair_ref[pl.ds(t, 1), :]
            for c in range(9):
                kept = jnp.where(named, spread[c * half : (c + 1) * half], 0.0)
                entry_ref[c, pl.ds(t, 1), :] = jnp.sum(kept, axis=0, keepdims=True)
        return 0

    lax.fori_loop(0, tiles // unrolls[0], fetch, 0)
    cx, cy = entry_ref[0] - 0.5, entry_ref[1] - 0.5
    a, b, c2 = entry_ref[2], entry_ref[3], entry_ref[4]
    opacity = 1.0 / (1.0 + jnp.exp(-entry_ref[8]))
    ax, ay = a * cx + b * cy, b * cx + c2 * cy
    base = jnp.log(0.99 * opacity) * LOG2E - (0.5 * LOG2E) * (ax * cx + ay * cy)
    coefs = [
        (-0.5 * LOG2E) * a,
        -LOG2E * b,
        (-0.5 * LOG2E) * c2,
        LOG2E * ax,
        LOG2E * ay,
        jnp.where(pair_ref[...] >= 0, base, -400.0),
    ]
    for i, coef in enumerate(coefs):
        coef_ref[:, i, :] = coef
    coef_ref[:, 6, :] = jnp.zeros_like(a)
    coef_ref[:, 7, :] = jnp.zeros_like(a)

    def scans(arrays, triangle):
        parts = [part for array in arrays for part in split2(array)]
        done = dot_nn(jnp.concatenate(parts, 0), triangle)
        pieces = [done[i * K : (i + 1) * K] for i in range(len(parts))]
        return [high + low for high, low in zip(pieces[0::2], pieces[1::2])]

    def shade(g, _):
        several = [unrolls[1] * g + i for i in range(unrolls[1])]
        blank, pad = jnp.zeros((8, K), BF16), jnp.zeros((4, K), F32)
        exponents = [
            dot_nn(pixel_columns, jnp.concatenate([*split3(coef_ref[t]), blank], 0))
            for t in several
        ]
        slopes, cot_rows = [], []
        for t in several:
            cot_high, cot_low = split2(cot_ref[t])
            ch, cl = cot_high.astype(F32), cot_low.astype(F32)
            cot_columns = jnp.concatenate([ch, ch, cl, cl, pad], 0).T.astype(BF16)
            colors = jnp.concatenate([entry_ref[c, pl.ds(t, 1), :] for c in range(5, 8)], 0)
            color_high, color_low = split2(colors)
            kh, kl = color_high.astype(F32), color_low.astype(F32)
            color_rows = jnp.concatenate([kh, kl, kh, kl, pad], 0).astype(BF16)
            slopes.append(dot_nn(cot_columns, color_rows))
            cot_rows.append(jnp.concatenate([ch, cl, pad[0:2]], 0).astype(BF16))
        alphas = [jnp.exp2(exponent) for exponent in exponents]
        log_keeps = [jnp.log(1.0 - alpha) for alpha in alphas]
        prefixes = scans(log_keeps, dots_ref[0:K])
        weights = [jnp.exp(prefix) * alpha for prefix, alpha in zip(prefixes, alphas)]
        pulls = [weight * slope for weight, slope in zip(weights, slopes)]
        suffixes = scans(pulls, dots_ref[K : 2 * K])
        for t, weight, rows in zip(several, weights, cot_rows):
            both = jnp.concatenate(split2(weight), 0)
            sums_ref[t, 8:16, :] = dot_nn(jnp.concatenate([rows, rows], 1), both)
        mass = jnp.concatenate([monomials, monomials], 1)
        for t, alpha, log_keep, pull, suffix in zip(several, alphas, log_keeps, pulls, suffixes):
            q = pull - alpha * jnp.exp(-log_keep) * suffix
            sums_ref[t, 0:8, :] = dot_nn(mass, jnp.concatenate(split2(q), 0))
        return 0

    lax.fori_loop(0, tiles // unrolls[1], shade, 0)
    mxx, mxy, myy, mx, my, m0 = [sums_ref[:, i, :] for i in range(6)]
    sx, sy = mx - cx * m0, my - cy * m0
    entry_ref[0] = a * sx + b * sy
    entry_ref[1] = b * sx + c2 * sy
    entry_ref[2] = -0.5 * (mxx - cx * (mx + sx))
    entry_ref[3] = -(mxy - cx * my - cy * sx)
    entry_ref[4] = -0.5 * (myy - cy * (my + sy))
    for i in range(3):
        entry_ref[5 + i] = sums_ref[:, 8 + i, :] + sums_ref[:, 11 + i, :]
    entry_ref[8] = (1.0 - opacity) * m0

    def give(g, _):
        sides, hots = [], []
        for i in range(unrolls[2]):
            t = unrolls[2] * g + i
            hot = hot_place(t)
            hits = hits16(half, pair_ref[pl.ds(t, 1), :])
            placed = []
            for c in range(9):
                high, low = split2(entry_ref[c, pl.ds(t, 1), :])
                placed.append(jnp.concatenate([keep16(hits, high), keep16(hits, low)], 1))
            sides.append(jnp.concatenate(placed, 0))
            hots += [hot, hot]
        grad_ref[...] += dot_nt(jnp.concatenate(sides, 1), jnp.concatenate(hots, 1))
        return 0

    lax.fori_loop(0, tiles // unrolls[2], give, 0)
    for c in range(9):
        part = grad_ref[c * half : (c + 1) * half, :]
        out_ref[pl.ds(c, half, stride=18), :] = part[:, :LANES]
        out_ref[pl.ds(9 + c, half, stride=18), :] = part[:, LANES:]


def collect(packed_ref, ends_ref, vals_ref, first, number, held_ref):
    owners = vals_ref.shape[0] // 9
    totals = to_scalars(packed_ref[owners + 1 : owners + 2, 0 : 2 * owners], ends_ref)
    base = owners * LANES - totals[1]
    held_ref[...] = jnp.zeros_like(held_ref)
    blank = jnp.zeros((8 - number, LANES), F32)

    def row_at(g, j):
        rows = vals_ref[pl.ds(pl.multiple_of(g * 72, 8), 72), :]
        at = 9 * j + first
        return jnp.concatenate([rows[at : at + number], blank], 0)

    def store(bucket, at, block):
        held_ref[bucket, pl.ds(at, 1), :, :] = block[None]

    compact(owners, ends_ref, base, row_at, store)
    return totals


def collect_kernel(packed_ref, vals_ref, look_ref, held_ref, ends_ref):
    collect(packed_ref, ends_ref, vals_ref, 5, 4, held_ref)
    look_ref[...] = held_ref[0, :, 0:4, :] + held_ref[1, :, 0:4, :]


def add_chunks(ids_ref, value_refs, totals, owners, acc_ref, transposed=False):
    def chunk(row, bucket, wide):
        sides, hots = [], []
        for at in range(0, wide, 2):
            first = row + at
            ids = ids_row(ids_ref, first)
            hot = hot_rows(ids, bucket)
            hits = hits16(LOW, ids & (LOW - 1))
            stacked = []
            for ref, number in value_refs[bucket]:
                for c in range(number):
                    pair = jnp.concatenate(
                        [ref[first, c : c + 1, :], ref[first + 1, c : c + 1, :]], 1
                    )
                    high, low = split2(pair)
                    stacked.append(
                        jnp.concatenate([keep16(hits, high), keep16(hits, low)], 1)
                    )
            sides.append(jnp.concatenate(stacked, 0))
            hots += [hot, hot]
        side, hot = jnp.concatenate(sides, 1), jnp.concatenate(hots, 1)
        if transposed:
            acc_ref[bucket] += dot_nt(hot, side)
        else:
            acc_ref[bucket] += dot_nt(side, hot)

    each_chunk(totals, owners, chunk)


def scatter_kernel(
    ids_ref, vals_ref, look_vals_ref, geo_ref, look_acc_ref, acc_ref, held_ref, ends_ref
):
    owners = vals_ref.shape[0] // 9
    totals = collect(ids_ref, ends_ref, vals_ref, 0, 5, held_ref)
    acc_ref[...] = jnp.zeros_like(acc_ref)
    values = [[(held_ref.at[bucket], 5), (look_vals_ref, 4)] for bucket in range(2)]
    add_chunks(ids_ref, values, totals, owners, acc_ref)
    for c in range(5):
        at = slice(c * LOW, (c + 1) * LOW)
        geo_ref[c] = jnp.concatenate([acc_ref[0, at], acc_ref[1, at]], 0).T
    for bucket in range(2):
        look_acc_ref[bucket] = acc_ref[bucket, 5 * LOW :, :].T


def add_view(ids_ref, vals_ref, start_ref, acc_ref):
    owners = vals_ref.shape[0] - 1
    place = ids_ref[owners + 1 : owners + 2, :]
    acc_ref[...] = start_ref[...]
    totals = place[0, owners - 1], place[0, 2 * owners - 1]
    add_chunks(ids_ref, [[(vals_ref, 4)]] * 2, totals, owners, acc_ref, transposed=True)


def finish_kernel(ids_ref, vals_ref, start_ref, look_ref, acc_ref):
    add_view(ids_ref, vals_ref, start_ref, acc_ref)
    for c in range(4):
        at = slice(c * LOW, (c + 1) * LOW)
        look_ref[:, c, :] = jnp.concatenate([acc_ref[0, :, at], acc_ref[1, :, at]], 1)


HBM = pl.BlockSpec(memory_space=pltpu.HBM)
VMEM = pl.BlockSpec(memory_space=pltpu.VMEM)
SMEM = pl.BlockSpec(memory_space=pltpu.SMEM)
LIMIT = pltpu.CompilerParams(vmem_limit_bytes=40 * 1024 * 1024)


def exchange(values, owners, axis="owner"):
    sent = values.reshape(owners, 1, -1)
    got = lax.all_to_all(sent, axis, split_axis=0, concat_axis=0, tiled=True)
    return got.reshape(values.shape)


def shards(geometry, appearance, list_owner, list_local, counts, cotangent):
    owners = lax.axis_size("owner")
    views = lax.axis_size("view")
    tiles = counts.shape[1]
    gauss = geometry.shape[2]
    rows = gauss // LANES
    target = list_owner.reshape(1, tiles * K)
    requests, pairs, places = pl.pallas_call(
        plan_kernel,
        out_shape=(
            jax.ShapeDtypeStruct((owners, LANES), jnp.int32),
            jax.ShapeDtypeStruct((tiles, K), jnp.int32),
            jax.ShapeDtypeStruct((tiles, K), jnp.int32),
        ),
        in_specs=[HBM, HBM, HBM],
        out_specs=(VMEM, VMEM, VMEM),
        scratch_shapes=[
            pltpu.SMEM((1, tiles), jnp.int32),
            pltpu.VMEM((1, tiles * K), jnp.int32),
            pltpu.VMEM((1, tiles * K), jnp.int32),
            pltpu.SemaphoreType.DMA((3,)),
        ],
        compiler_params=pltpu.CompilerParams(vmem_limit_bytes=60 * 1024 * 1024),
    )(counts, target, list_local)
    table = pl.pallas_call(
        table_kernel,
        out_shape=jax.ShapeDtypeStruct((2, 9 * LOW, 512), BF16),
        in_specs=[VMEM, VMEM],
        out_specs=VMEM,
        compiler_params=LIMIT,
    )(geometry.reshape(5, rows, LANES), appearance.reshape(4, rows, LANES))
    asked = exchange(requests, owners)
    picked, packed = pl.pallas_call(
        gather_kernel,
        out_shape=(
            jax.ShapeDtypeStruct((owners * 9, LANES), F32),
            jax.ShapeDtypeStruct((owners + 8, LANES), jnp.int32),
        ),
        in_specs=[VMEM, VMEM],
        out_specs=(VMEM, VMEM),
        scratch_shapes=[
            pltpu.SMEM((8, LANES), jnp.int32),
            pltpu.VMEM((2, owners + 8, LANES), jnp.int32),
            pltpu.VMEM((2, owners + 2, 16, LANES), F32),
        ],
        compiler_params=LIMIT,
    )(asked, table)
    fetched = exchange(picked, owners)
    shifts = [[(i, (i + k) % views) for i in range(views)] for k in range(1, views)]
    other_ids = [lax.ppermute(packed, "view", shift) for shift in shifts]
    fetched, other_ids = lax.optimization_barrier((fetched, other_ids))
    outgoing = pl.pallas_call(
        functools.partial(tile_kernel, (16, 8, 16)),
        out_shape=jax.ShapeDtypeStruct((owners * 9, LANES), F32),
        in_specs=[VMEM, VMEM, VMEM, VMEM],
        out_specs=VMEM,
        scratch_shapes=[
            pltpu.VMEM((9 * owners // 2, 4 * LANES), BF16),
            pltpu.VMEM((9 * owners // 2, 2 * LANES), F32),
            pltpu.VMEM((2 * K, K), BF16),
            pltpu.VMEM((9, tiles, K), F32),
            pltpu.VMEM((tiles, 8, K), F32),
            pltpu.VMEM((tiles, 16, K), F32),
        ],
        compiler_params=LIMIT,
    )(pairs, places, cotangent[0], fetched)
    returned = exchange(outgoing, owners)
    look_vals = pl.pallas_call(
        collect_kernel,
        out_shape=jax.ShapeDtypeStruct((owners + 1, 4, LANES), F32),
        in_specs=[VMEM, VMEM],
        out_specs=VMEM,
        scratch_shapes=[
            pltpu.VMEM((2, owners + 1, 8, LANES), F32),
            pltpu.SMEM((8, LANES), jnp.int32),
        ],
        compiler_params=LIMIT,
    )(packed, returned)
    other_vals = [lax.ppermute(look_vals, "view", shift) for shift in shifts]
    sums = jax.ShapeDtypeStruct((2, 256, 4 * LOW), F32)
    geo, look = pl.pallas_call(
        scatter_kernel,
        out_shape=(jax.ShapeDtypeStruct((5, rows, LANES), F32), sums),
        in_specs=[VMEM, VMEM, VMEM],
        out_specs=(VMEM, VMEM),
        scratch_shapes=[
            pltpu.VMEM((2, 9 * LOW, 256), F32),
            pltpu.VMEM((2, owners + 1, 8, LANES), F32),
            pltpu.SMEM((8, LANES), jnp.int32),
        ],
        compiler_params=LIMIT,
    )(packed, returned, look_vals)
    for i in reversed(range(views - 1)):
        last = i == 0
        look = pl.pallas_call(
            finish_kernel if last else add_view,
            out_shape=jax.ShapeDtypeStruct((rows, 4, LANES), F32) if last else sums,
            in_specs=[VMEM, VMEM, VMEM],
            out_specs=VMEM,
            scratch_shapes=[pltpu.VMEM((2, 256, 4 * LOW), F32)] if last else [],
            compiler_params=LIMIT,
        )(other_ids[i], other_vals[i], look)
    look = jnp.transpose(look, (1, 0, 2)).reshape(4, gauss)
    return (geo.reshape(1, 5, gauss), look)


def solution(mesh):
    placed = (
        P("view", None, "owner"),
        P(None, "owner"),
        P("view", "owner", None),
        P("view", "owner"),
        P("view", "owner"),
        P("view", "owner", None, None),
    )
    return jax.shard_map(
        shards,
        mesh=mesh,
        in_specs=placed,
        out_specs=(P("view", None, "owner"), P(None, "owner")),
        check_vma=False,
    )
```
